256 devices in a mesh: dp: 16 (over z, core), expert: 16 (over x, y).
Axes of the slice: x: 4, y: 4, z: 8, core: 2. Of those that a mesh axis runs over, the one named last changes fastest.
Arguments:
- attn_rows: bfloat16 [98304, 2048], P(('dp', 'expert')), may hold values from -6 to 6
- out_grad: bfloat16 [98304, 2048], P(('dp', 'expert')), may hold values from -1.5 to 1.5
- owner_rows: int32 [16, 16], P('expert'), may hold values from 1 to 384, 4096 in all within a row
- routes: int32 [65536, 1], P(('dp', 'expert')), may hold values from 0 to 15; in each aligned block of 256 rows (0 to 255, 256 to 511, ...) at most 24 rows name the same one
- gates: bfloat16 [65536], P(('dp', 'expert')), may hold values from 0.25 to 1
- gate_weight: bfloat16 [16, 2048, 768], P('expert', 'dp'), may hold values from -0.125 to 0.125
- up_weight: bfloat16 [16, 2048, 768], P('expert', 'dp'), may hold values from -0.125 to 0.125
- down_weight: bfloat16 [16, 2048, 768], P('expert', 'dp'), may hold values from -0.21875 to 0.21875
Outputs:
- moe_out: bfloat16 [65536, 2048], P(('dp', 'expert'))
- in_grad: bfloat16 [65536, 2048], P(('dp', 'expert'))
- grad_gate: float32 [16, 2048, 768], P('expert', 'dp')
- grad_up: float32 [16, 2048, 768], P('expert', 'dp')
- grad_down: float32 [16, 2048, 768], P('expert', 'dp')
The draws below stay inside these ranges and needn't reach their ends.
Inputs may be any that keep to these rules, and one draw needn't show every extreme that they name: `owner_rows`: each row sums to 4096, and the largest entry of each row is exactly 384. `routes`: within the 256 rows of one device no expert is named by more than 24 rows, and in some devices' rows some expert is named by exactly 24.
All inputs are finite; a program needn't handle non-finite values.
Results may differ from the reference program's by a relative error of at most 0.02.
Values may be sent and summed in bfloat16 or wider, within the bound.
A program may use at most 128 MiB of HBM per device.

```python
import math
import jax
import jax.numpy as jnp
import numpy as np
from jax import lax

D = 2048
FF = 768
TOK_DEV = 256
EXPERTS = 16
CAP = 24
ATT_CAP = 384
TOKENS = 65536
N_DP = 16
N_EXPERT = 16


def block_scale(own_key, extent, pieces, least, largest):
    gain = 1.0
    for dim, blocks in pieces:
        draws = jax.random.uniform(jax.random.fold_in(jax.random.fold_in(own_key, 6), dim), (blocks,), jnp.float32, least / len(pieces), largest / len(pieces))
        gain = gain * jnp.repeat(jnp.exp(draws), extent[dim] // blocks).reshape((-1,) + (1,) * (len(extent) - 1 - dim))
    return gain


def length_profile(number_of, total, most, slope):
    portions = [(1 << 20) // math.isqrt(rank ** slope) + 1 for rank in range(2, number_of + 1)]
    rest, holding = total - most - (number_of - 1), [1] * (number_of - 1)
    while rest > 0:
        free = [i for i in range(number_of - 1) if holding[i] < most]
        mass, budget = sum([portions[i] for i in free]), rest
        for i in free:
            more = min(most - holding[i], max(1, budget * portions[i] // mass), rest)
            holding[i] = holding[i] + more
            rest = rest - more
    return np.array([most] + holding)


def ragged(key, count, total, limit, lean):
    if count == 2:
        one = jax.random.randint(key, (), max(1, total - limit), min(limit, total - 1) + 1)
        return jnp.stack([one, total - one])
    tallies = jnp.asarray(length_profile(count, total, limit, lean), jnp.int32)
    pairs = (count - 1) // 2
    source_of, sink = tallies[1:1 + 2 * pairs:2], tallies[2:2 + 2 * pairs:2]
    room = jnp.minimum(source_of - 1, limit - sink)
    passed = jax.random.randint(jax.random.fold_in(key, 1), (pairs,), 0, 1 << 20) % (room + 1)
    tallies = tallies.at[1:1 + 2 * pairs:2].set(source_of - passed).at[2:2 + 2 * pairs:2].set(sink + passed)
    return tallies[jax.random.permutation(jax.random.fold_in(key, 2), count)]


def assign_block(own_key, own, number, rows, number_of, top, most, slope):
    sequence = jax.random.permutation(own_key, number_of)
    heavy_load, common = shares(number_of, rows * top, most, slope, True), shares(number_of, rows * top, most, slope, False)
    places = jnp.arange(number_of)

    def named(lengths, offset_by):
        used = int((lengths > 0).sum())
        fixed = max(1, used // 4)
        moved = fixed + (places - fixed + offset_by * (used - fixed)) % max(1, number_of - fixed)
        return jnp.zeros((number_of,), jnp.int32).at[sequence[jnp.where(places < fixed, places, moved)]].set(jnp.asarray(lengths, jnp.int32))

    lengths = jnp.where(number % 4 == 0, named(heavy_load, number // 4), named(common, number - number // 4 - 1))
    mixed = jax.random.permutation(jax.random.fold_in(own, 3), number_of)
    giver, receiver = mixed[0:number_of // 2 * 2:2], mixed[1:number_of // 2 * 2:2]
    slack = jnp.minimum(lengths[giver] - 1, most - lengths[receiver]) // 2
    slack = jnp.where((giver == sequence[0]) | (receiver == sequence[0]) | (lengths[receiver] == 0), 0, jnp.maximum(slack, 0))
    moved = jax.random.randint(jax.random.fold_in(own, 4), (number_of // 2,), 0, 1 << 20) % (slack + 1)
    lengths = lengths.at[giver].add(-moved).at[receiver].add(moved)
    members = jnp.searchsorted(jnp.cumsum(lengths), jnp.arange(rows * top), side="right").astype(jnp.int32)
    grid = members.reshape(top, rows).T
    grid = grid[jax.random.permutation(jax.random.fold_in(own, 1), rows)]
    offset_by = jax.random.randint(jax.random.fold_in(own, 2), (rows, 1), 0, top)
    return jnp.take_along_axis(grid, (jnp.arange(top)[None, :] + offset_by) % top, axis=1)


def shares(amount, total, limit, slope, full):
    weights = [(1 << 20) // math.isqrt(rank ** slope) + 1 for rank in range(1, amount + 1)]
    largest = limit if full else min(limit, max(-(-total // amount), total * weights[0] // sum(weights)))
    least = 1 if total - largest >= amount - 1 else 0
    counts, rest = [largest] + [least] * (amount - 1), total - largest - least * (amount - 1)
    while rest > 0:
        movable = [i for i in range(1, amount) if counts[i] < largest] or [i for i in range(1, amount) if counts[i] < limit]
        pool, left = sum([weights[i] for i in movable]), rest
        for i in movable:
            addition = min(limit - counts[i], max(1, left * weights[i] // pool), rest)
            counts[i] = counts[i] + addition
            rest = rest - addition
    return np.array(counts)


def bell_draw(rng, dims, deviation, bound, cuts=(), held_as=jnp.bfloat16):
    result = jax.random.normal(rng, dims, jnp.float32) * deviation
    if len(cuts) > 0:
        result = block_scale(rng, dims, cuts, -0.22, 0.18) * result
    return jnp.clip(result, min=-bound, max=bound).astype(held_as)


def setup_inputs(seed: int = 0) -> dict:
    arg_keys = jax.random.split(jax.random.key(seed), 9)
    attn_rows = bell_draw(arg_keys[0], (N_DP * N_EXPERT * ATT_CAP, D), 1.0, 6.0, ((0, 256),))
    out_grad = bell_draw(arg_keys[1], (N_DP * N_EXPERT * ATT_CAP, D), 0.25, 1.5, ((0, 256),))
    owner_rows = jax.vmap(lambda own: ragged(own, N_DP, N_DP * TOK_DEV, ATT_CAP, 2))(jax.random.split(arg_keys[2], N_EXPERT)).reshape((N_EXPERT, N_DP)).astype(jnp.int32)
    routes_keys = jax.random.split(jax.random.fold_in(arg_keys[3], 1), TOKENS // TOK_DEV)
    routes_turns = jax.random.permutation(jax.random.fold_in(arg_keys[3], 3), TOKENS // TOK_DEV)
    routes = jax.vmap(lambda own, number: assign_block(jax.random.fold_in(arg_keys[3], 2), own, number, TOK_DEV, EXPERTS, 1, CAP, 2))(routes_keys, routes_turns).reshape((TOKENS, 1))
    gates = jnp.clip(0.25 + 0.75 * jax.random.uniform(arg_keys[4], (TOKENS,), jnp.float32) ** block_scale(arg_keys[4], (TOKENS,), ((0, 256),), -0.2, 0.2), 0.25, 1.0).astype(jnp.bfloat16)
    gate_weight = bell_draw(arg_keys[5], (EXPERTS, D, FF), D ** -0.5, 0.125, ((0, 16), (1, 16)))
    up_weight = bell_draw(arg_keys[6], (EXPERTS, D, FF), D ** -0.5, 0.125, ((0, 16), (1, 16)))
    down_weight = bell_draw(arg_keys[7], (EXPERTS, D, FF), FF ** -0.5, 0.21875, ((0, 16), (1, 16)))
    return dict(attn_rows=attn_rows, out_grad=out_grad, owner_rows=owner_rows, routes=routes, gates=gates, gate_weight=gate_weight, up_weight=up_weight, down_weight=down_weight)


def relayout(values, owner_rows):
    row_ends = jnp.cumsum(owner_rows, axis=1).astype(jnp.int32)
    row_starts = (row_ends - owner_rows).astype(jnp.int32)
    positions = jnp.arange(N_DP * TOK_DEV, dtype=jnp.int32)
    owner_of = jnp.sum((row_ends[:, None, :] <= positions[None, :, None]).astype(jnp.int32), axis=2).astype(jnp.int32)
    owner_start = jnp.take_along_axis(row_starts, owner_of, axis=1)
    group_iota = jnp.arange(N_EXPERT, dtype=jnp.int32)[:, None]
    flat_index = ((owner_of * N_EXPERT + group_iota) * ATT_CAP + positions[None, :] - owner_start).astype(jnp.int32)
    picked = jnp.take(values, flat_index.reshape(-1), axis=0)
    picked = picked.reshape(N_EXPERT, TOK_DEV, N_DP, D)
    return jnp.transpose(picked, (2, 0, 1, 3))


def slot_table(route_col):
    expert_iota = jnp.arange(EXPERTS, dtype=jnp.int32)
    onehot = (route_col[:, None] == expert_iota[None, :]).astype(jnp.int32)
    before = (jnp.cumsum(onehot, axis=0) - onehot).astype(jnp.int32)
    rank_in = jnp.sum(before * onehot, axis=1).astype(jnp.int32)
    slot_index = (route_col * CAP + rank_in).astype(jnp.int32)
    source = jnp.full((EXPERTS * CAP,), TOK_DEV, dtype=jnp.int32)
    source = source.at[slot_index].set(jnp.arange(TOK_DEV, dtype=jnp.int32))
    return slot_index, source


def by_expert(values, source):
    pad_shape = (values.shape[0], 1) + values.shape[2:]
    padded = jnp.concatenate([values, jnp.zeros(pad_shape, values.dtype)], axis=1)
    indices = source.reshape(source.shape + (1,) * (values.ndim - 2))
    picked = jnp.take_along_axis(padded, indices, axis=1)
    picked = picked.reshape((N_EXPERT, EXPERTS, CAP) + values.shape[2:])
    picked = jnp.swapaxes(picked, 0, 1)
    return picked.reshape((EXPERTS, N_EXPERT * CAP) + values.shape[2:])


def to_sources(values, slot_index):
    back = values.reshape(EXPERTS, N_EXPERT, CAP, D)
    back = jnp.swapaxes(back, 0, 1).reshape(N_EXPERT, EXPERTS * CAP, D)
    return jnp.take_along_axis(back, slot_index[:, :, None], axis=1)


def expert_block(rows_in, grads_in, scales, w_gate, w_up, w_down):
    gate_pre = jnp.dot(rows_in, w_gate, preferred_element_type=jnp.float32)
    up_pre = jnp.dot(rows_in, w_up, preferred_element_type=jnp.float32)
    sigmoid_g = jax.nn.sigmoid(gate_pre)
    active = gate_pre * sigmoid_g
    hidden = (active * up_pre).astype(jnp.bfloat16)
    factor = scales.astype(jnp.float32)[:, None]
    produced = jnp.dot(hidden, w_down.T, preferred_element_type=jnp.float32)
    expert_out = (factor * produced).astype(jnp.bfloat16)
    out_cot = (factor * grads_in.astype(jnp.float32)).astype(jnp.bfloat16)
    hidden_cot = jnp.dot(out_cot, w_down, preferred_element_type=jnp.float32)
    gate_cot = (hidden_cot * up_pre * sigmoid_g * (1.0 + gate_pre * (1.0 - sigmoid_g))).astype(jnp.bfloat16)
    up_cot = (hidden_cot * active).astype(jnp.bfloat16)
    row_cot = jnp.dot(gate_cot, w_gate.T, preferred_element_type=jnp.float32)
    row_cot = (row_cot + jnp.dot(up_cot, w_up.T, preferred_element_type=jnp.float32)).astype(jnp.bfloat16)
    term_gate = jnp.dot(rows_in.T, gate_cot, preferred_element_type=jnp.float32).astype(jnp.bfloat16)
    term_up = jnp.dot(rows_in.T, up_cot, preferred_element_type=jnp.float32).astype(jnp.bfloat16)
    term_down = jnp.dot(out_cot.T, hidden, preferred_element_type=jnp.float32).astype(jnp.bfloat16)
    return expert_out, row_cot, term_gate, term_up, term_down


def apply_expert(inputs):
    return expert_block(*inputs)


def reference(attn_rows, out_grad, owner_rows, routes, gates, gate_weight, up_weight, down_weight):
    moe_rows = relayout(attn_rows, owner_rows)
    moe_grads = relayout(out_grad, owner_rows)
    route_grid = routes.reshape(N_DP, N_EXPERT, TOK_DEV)
    gate_grid = gates.reshape(N_DP, N_EXPERT, TOK_DEV)

    def one_row(totals, inputs):
        rows_d, grads_d, route_d, scale_d = inputs
        slot_index, source = jax.vmap(slot_table)(route_d)
        rows_x = by_expert(rows_d, source)
        rows_y = by_expert(grads_d, source)
        rows_c = by_expert(scale_d, source)
        results = lax.map(apply_expert, (rows_x, rows_y, rows_c, gate_weight, up_weight, down_weight))
        out_rows = to_sources(results[0], slot_index)
        cot_rows = to_sources(results[1], slot_index)
        totals = (totals[0] + results[2].astype(jnp.float32),
                  totals[1] + results[3].astype(jnp.float32),
                  totals[2] + results[4].astype(jnp.float32))
        return totals, (out_rows, cot_rows)

    zero_sum = jnp.zeros((EXPERTS, D, FF), jnp.float32)
    totals, (out_all, cot_all) = lax.scan(one_row, (zero_sum, zero_sum, zero_sum), (moe_rows, moe_grads, route_grid, gate_grid))
    return out_all.reshape(TOKENS, D), cot_all.reshape(TOKENS, D), totals[0], totals[1], totals[2]
```

```python
import jax
import jax.numpy as jnp
from jax import lax
from jax.experimental import pallas as pl
from jax.experimental.pallas import tpu as pltpu
from jax.sharding import PartitionSpec as P

MESH = pl.DeviceIdType.MESH
BF = jnp.bfloat16
F32 = jnp.float32
N = 16
Z = 8
CAP = 24
CH = 2 * CAP
HALF = 1024
ROWS = N * CAP
STK = 2 * ROWS
TOK = 256
D = 2048
FF = 768
SH = 128
GATE, UP, DOWN = 0, 1, 2


def nn(a, b):
    return jnp.dot(a, b, preferred_element_type=F32)


def nt(a, b):
    return lax.dot_general(a, b, (((1,), (1,)), ((), ())), preferred_element_type=F32)


def kernel(
    x_hbm, dy_hbm, lens, routes, gates, wg_hbm, wu_hbm, wd_hbm,
    out_hbm, dx_hbm, gg_hbm, gu_hbm, gd_hbm,
    xin, yin, xs, ys, gotx, goty, s2x, s2y, rcx, rcy, backo, backd,
    w, perm, perm_g, a_t, sel,
    xt, yt, xt_s, yt_s, hid, gcot, ucot, f1, f2, tmp, s4, sb, mo, gr,
    ld, rel_s, rel_r, ex_s, ex_r, bk_s, bk_r, ag_s, ag_r, sib_s, sib_r, act_s, act_r, rs_s, rs_r, st,
):
    dp = lax.axis_index("dp")
    ex = lax.axis_index("expert")
    z = dp // 2
    c = lax.rem(dp, 2)
    sibling = {"dp": dp + 1 - 2 * c}

    loads = []
    for i, (src, dst) in enumerate(((x_hbm, xin), (dy_hbm, yin))):
        for h in range(2):
            loads.append(pltpu.make_async_copy(
                src.at[:, pl.ds(h * HALF, HALF)], dst.at[pl.ds(h * ROWS, ROWS)], ld.at[2 * i + h]))
    my_rows = pl.multiple_of(dp * SH, SH)
    for i, src in enumerate((wg_hbm, wu_hbm, wd_hbm)):
        loads.append(pltpu.make_async_copy(src.at[0], w.at[i, pl.ds(my_rows, SH)], ld.at[4 + i]))
    for cp in loads:
        cp.start()

    bar = pltpu.get_barrier_semaphore()

    def greet(i, _):
        pl.semaphore_signal(bar, 1, device_id={"dp": lax.rem(dp + i, N)}, device_id_type=MESH)
        pl.semaphore_signal(bar, 1, device_id={"expert": lax.rem(ex + i, N)}, device_id_type=MESH)
        return 0

    lax.fori_loop(1, N, greet, 0)

    def prefix(i, acc):
        return acc + jnp.where(i < dp, lens[0, i], 0)

    start = lax.fori_loop(0, N, prefix, jnp.int32(0))
    col = lax.broadcasted_iota(jnp.int32, (1, STK), 1)
    right_half = (col >= ROWS).astype(jnp.int32)
    r = col - ROWS * right_half
    dest = ((r + start) & (N - 1)) * CH + CAP * right_half + (r >> 4)
    row_iota = lax.broadcasted_iota(jnp.int32, (STK, STK), 0)
    perm[...] = jnp.where(row_iota == dest, 1.0, 0.0).astype(BF)

    def permute(p_ref, src, dst):
        def body(t, _):
            cols = pl.ds(pl.multiple_of(t * 256, 256), 256)
            dst[:, cols] = nn(p_ref[...], src[:, cols]).astype(BF)
            return 0
        lax.fori_loop(0, HALF // 256, body, 0)

    def tile(i):
        return pl.ds(pl.multiple_of(i * CH, CH), CH)

    def scatter(src, dst, ssem, rsem, axis, me):
        def body(i, _):
            t = lax.rem(me + i, N)
            pltpu.make_async_remote_copy(
                src_ref=src.at[tile(t)], dst_ref=dst.at[tile(me)], send_sem=ssem, recv_sem=rsem,
                device_id={axis: t}, device_id_type=MESH).start()
            return 0
        lax.fori_loop(1, N, body, 0)
        dst[tile(me), :] = src[tile(me), :]

    def scatter_all(src, dst, ssem, rsem, axis):
        me = dp if axis == "dp" else ex
        span = pl.ds(0, (N - 1) * CH)
        return pltpu.make_async_remote_copy(
            src_ref=src.at[span], dst_ref=dst.at[span], send_sem=ssem, recv_sem=rsem,
            device_id={axis: lax.rem(me + 1, N)}, device_id_type=MESH)

    def shard(o, lo=0, n=SH):
        return pl.ds(pl.multiple_of((2 * o + c) * SH + lo, 64), n)

    def span_of(hop, way):
        if hop < 4:
            return 0, SH
        return (0 if way == 0 else 64), 64

    def chip(k):
        return lax.rem(z + k + 2 * Z, Z)

    def ag(i, way, hop):
        sign = 1 - 2 * way
        lo, n = span_of(hop, way)
        rows = shard(chip(-sign * (hop - 1)), lo, n)
        return pltpu.make_async_remote_copy(
            src_ref=w.at[i, rows], dst_ref=w.at[i, rows], send_sem=ag_s.at[i, way, hop - 1],
            recv_sem=ag_r.at[i, way, hop - 1], device_id={"dp": 2 * chip(sign) + c}, device_id_type=MESH)

    def ag_in(i, way, hop):
        sign = 1 - 2 * way
        lo, n = span_of(hop, way)
        rows = shard(chip(-sign * hop), lo, n)
        return pltpu.make_async_remote_copy(
            src_ref=w.at[i, rows], dst_ref=w.at[i, rows], send_sem=ag_s.at[i, way, hop - 1],
            recv_sem=ag_r.at[i, way, hop - 1], device_id={"dp": 2 * chip(sign) + c}, device_id_type=MESH)

    def share(i, o):
        rows = shard(o)
        return pltpu.make_async_remote_copy(
            src_ref=w.at[i, rows], dst_ref=w.at[i, rows], send_sem=sib_s.at[i], recv_sem=sib_r.at[i],
            device_id=sibling, device_id_type=MESH)

    def shared_all(i):
        rows = pl.ds(0, Z * SH)
        return pltpu.make_async_remote_copy(
            src_ref=w.at[i, rows], dst_ref=w.at[i, rows], send_sem=sib_s.at[i], recv_sem=sib_r.at[i],
            device_id=sibling, device_id_type=MESH)

    def ag_step(i, hop):
        for way in range(2):
            ag_in(i, way, hop).wait_recv()
            if hop < 4:
                ag(i, way, hop + 1).start()
                share(i, chip((2 * way - 1) * hop)).start()
        if hop == 4:
            share(i, chip(4)).start()

    loads[0].wait()
    loads[1].wait()
    permute(perm, xin, xs)
    pl.semaphore_wait(bar, 2 * (N - 1))
    scatter(xs, gotx, rel_s.at[0], rel_r.at[0], "dp", dp)
    loads[2].wait()
    loads[3].wait()
    permute(perm, yin, ys)
    scatter(ys, goty, rel_s.at[1], rel_r.at[1], "dp", dp)
    for i in range(3):
        loads[4 + i].wait()
        ag(i, 0, 1).start()
        ag(i, 1, 1).start()
        share(i, z).start()

    expert_iota = lax.broadcasted_iota(jnp.int32, (N, TOK), 0)
    route = routes[...]
    hot = expert_iota == route
    hot_f = jnp.where(hot, 1.0, 0.0)
    earlier = (lax.broadcasted_iota(jnp.int32, (TOK, TOK), 0) < lax.broadcasted_iota(jnp.int32, (TOK, TOK), 1))
    before = nn(hot_f.astype(BF), jnp.where(earlier, 1.0, 0.0).astype(BF))
    rank = jnp.sum(before * hot_f, axis=0, keepdims=True).astype(jnp.int32)
    slot = route * CH + rank
    pos = N * lax.broadcasted_iota(jnp.int32, (1, TOK), 1) + dp
    owner = jnp.zeros((1, TOK), jnp.int32)
    first = jnp.zeros((1, TOK), jnp.int32)
    end = jnp.int32(0)
    for b in range(N):
        end = end + lens[0, b]
        past = pos >= end
        owner = owner + jnp.where(past, 1, 0)
        first = jnp.where(past, end, first)
    got_row = owner * CH + ((pos - first) >> 4)
    gate_f = gates[...].astype(F32)
    tall = lax.broadcasted_iota(jnp.int32, (STK, TOK), 0)
    eye = jnp.where(
        lax.broadcasted_iota(jnp.int32, (TOK, TOK), 0) == lax.broadcasted_iota(jnp.int32, (TOK, TOK), 1), 1.0, 0.0
    ).astype(BF)
    for h in range(2):
        cols = pl.ds(h * TOK, TOK)
        hit = tall == slot + h * CAP
        plain = jnp.where(hit, 1.0, 0.0).astype(BF)
        gated = jnp.where(hit, gate_f, 0.0).astype(BF)
        a_t[0, :, cols] = plain
        a_t[1, :, cols] = gated
        a_t[2, :, cols] = jnp.where(tall == got_row + h * CAP, 1.0, 0.0).astype(BF)
        sel[0, h] = nt(eye, gated).astype(BF)
        sel[1, h] = nt(eye, plain).astype(BF)

    def build(t, _):
        rows = pl.ds(pl.multiple_of(t * 256, 256), 256)
        perm[rows, :] = nt(a_t[0, rows, :], a_t[2]).astype(BF)
        perm_g[rows, :] = nt(a_t[1, rows, :], a_t[2]).astype(BF)
        return 0

    lax.fori_loop(0, STK // 256, build, 0)

    scatter_all(xs, gotx, rel_s.at[0], rel_r.at[0], "dp").wait_recv()
    permute(perm, gotx, s2x)
    scatter(s2x, rcx, ex_s.at[0], ex_r.at[0], "expert", ex)
    for i in range(3):
        ag_step(i, 1)
    scatter_all(ys, goty, rel_s.at[1], rel_r.at[1], "dp").wait_recv()
    permute(perm_g, goty, s2y)
    scatter(s2y, rcy, ex_s.at[1], ex_r.at[1], "expert", ex)
    for i in range(3):
        ag_step(i, 2)

    def unstack(src, dst):
        def body(t, _):
            one = src[tile(2 * t), :].astype(F32)
            two = src[tile(2 * t + 1), :].astype(F32)
            at = pl.multiple_of(t * CH, CH)
            dst[pl.ds(at, CH), :] = jnp.concatenate([one[:CAP], two[:CAP]], axis=0).astype(BF)
            dst[pl.ds(at + ROWS, CH), :] = jnp.concatenate([one[CAP:], two[CAP:]], axis=0).astype(BF)
            return 0
        lax.fori_loop(0, N // 2, body, 0)

    own_rows = pl.ds(pl.multiple_of(c * ROWS, ROWS), ROWS)
    eye_s = eye[:SH, :SH]

    def turn(src, mine, theirs):
        def body(t, _):
            for par, dst in ((c, None), (1 - c, theirs)):
                d = 2 * t + par
                block = src[pl.ds(pl.multiple_of((d // Z) * ROWS, ROWS), ROWS),
                            pl.ds(pl.multiple_of(lax.rem(d, Z) * SH, SH), SH)]
                turned = nt(eye_s, block).astype(BF)
                if dst is None:
                    mine[t, :, own_rows] = turned
                else:
                    dst[t] = turned
            return 0
        lax.fori_loop(0, Z, body, 0)

    def give(i, src, dst):
        return pltpu.make_async_remote_copy(
            src_ref=src, dst_ref=dst, send_sem=act_s.at[i], recv_sem=act_r.at[i],
            device_id=sibling, device_id_type=MESH)

    gifts = (
        give(0, xt_s, xt.at[:, :, own_rows]),
        give(1, yt_s, yt.at[:, :, own_rows]),
        give(2, hid.at[own_rows], hid.at[own_rows]),
        give(3, gcot.at[own_rows], gcot.at[own_rows]),
        give(4, ucot.at[own_rows], ucot.at[own_rows]),
    )

    scatter_all(s2x, rcx, ex_s.at[0], ex_r.at[0], "expert").wait_recv()
    unstack(rcx, xin)
    turn(xin, xt, xt_s)
    gifts[0].start()
    for i in range(3):
        ag_step(i, 3)
    for i in range(3):
        ag_step(i, 4)
    shared_all(GATE).wait_recv()
    shared_all(UP).wait_recv()

    def forward(t, _):
        cols = pl.ds(pl.multiple_of(t * 256, 256), 256)
        g = nn(xin[:ROWS, :], w[GATE, :HALF, cols]) + nn(xin[ROWS:, :], w[GATE, HALF:, cols])
        u = nn(xin[:ROWS, :], w[UP, :HALF, cols]) + nn(xin[ROWS:, :], w[UP, HALF:, cols])
        sg = jax.nn.sigmoid(g)
        active = g * sg
        hid[own_rows, cols] = (active * u).astype(BF)
        f1[:, cols] = u * sg * (1.0 + g * (1.0 - sg))
        f2[:, cols] = active
        return 0

    lax.fori_loop(0, FF // 256, forward, 0)
    gifts[2].start()
    scatter_all(s2y, rcy, ex_s.at[1], ex_r.at[1], "expert").wait_recv()
    unstack(rcy, yin)
    turn(yin, yt, yt_s)
    gifts[1].start()

    def rs(i, way, hop):
        sign = 1 - 2 * way
        lo, n = span_of(hop, way)
        rows = pl.ds(lo, n)
        src = s4.at[i, rows] if hop == 4 else sb.at[i, way, hop, rows]
        return pltpu.make_async_remote_copy(
            src_ref=src, dst_ref=sb.at[i, way, hop - 1, rows], send_sem=rs_s.at[i, way, hop - 1],
            recv_sem=rs_r.at[i, way, hop - 1], device_id={"dp": 2 * chip(sign) + c}, device_id_type=MESH)

    def term(i, k):
        left = yt if i == DOWN else xt
        right = (gcot, ucot, hid)[i]
        return nn(left[chip(k)], right[...])

    def rs_step(i, hop):
        if hop == 4:
            s4[i] = term(i, 4).astype(BF)
            rs(i, 0, 4).start()
            rs(i, 1, 4).start()
            return
        if hop == 0:
            tmp[...] = term(i, 0)
            for way in range(2):
                rs(i, way, 1).wait_recv()
            gr[i] = tmp[...] + sb[i, 0, 0].astype(F32) + sb[i, 1, 0].astype(F32)
            return
        for way in range(2):
            tmp[...] = term(i, (1 - 2 * way) * hop)
            rs(i, way, hop + 1).wait_recv()
            lo, n = span_of(hop + 1, way)
            sb[i, way, hop, pl.ds(lo, n)] = (
                tmp[pl.ds(lo, n)] + sb[i, way, hop, pl.ds(lo, n)].astype(F32)).astype(BF)
            if n < SH:
                sb[i, way, hop, pl.ds(64 - lo, 64)] = tmp[pl.ds(64 - lo, 64)].astype(BF)
            rs(i, way, hop).start()

    gifts[1].wait_recv()
    gifts[2].wait_recv()
    rs_step(DOWN, 4)
    shared_all(DOWN).wait_recv()

    def backward(t, _):
        cols = pl.ds(pl.multiple_of(t * 256, 256), 256)
        hc = nn(yin[:ROWS, :], w[DOWN, :HALF, cols]) + nn(yin[ROWS:, :], w[DOWN, HALF:, cols])
        gcot[own_rows, cols] = (hc * f1[:, cols]).astype(BF)
        ucot[own_rows, cols] = (hc * f2[:, cols]).astype(BF)
        return 0

    lax.fori_loop(0, FF // 256, backward, 0)
    gifts[3].start()
    gifts[4].start()
    rs_step(DOWN, 3)

    def restack(first, second, dst, cols):
        for e in range(N):
            rows = slice(e * CAP, (e + 1) * CAP)
            dst[pl.ds(e * CH, CH), cols] = jnp.concatenate([first[rows], second[rows]], axis=0).astype(BF)

    scatter_all(xs, gotx, rel_s.at[0], rel_r.at[0], "dp").wait_send()
    scatter_all(ys, goty, rel_s.at[1], rel_r.at[1], "dp").wait_send()

    def produce(t, _):
        at = pl.multiple_of(t * 256, 256)
        left = hid[own_rows, :]
        restack(nt(left, w[DOWN, pl.ds(at, 256), :]), nt(left, w[DOWN, pl.ds(at + HALF, 256), :]),
                xs, pl.ds(at, 256))
        return 0

    lax.fori_loop(0, HALF // 256, produce, 0)
    scatter(xs, backo, bk_s.at[0], bk_r.at[0], "expert", ex)
    gifts[0].wait_recv()
    gifts[3].wait_recv()
    rs_step(GATE, 4)
    gifts[4].wait_recv()
    rs_step(UP, 4)

    def cotangent(t, _):
        at = pl.multiple_of(t * 256, 256)
        lg, lu = gcot[own_rows, :], ucot[own_rows, :]
        parts = []
        for h in range(2):
            rows = pl.ds(at + h * HALF, 256)
            parts.append(nt(lg, w[GATE, rows, :]) + nt(lu, w[UP, rows, :]))
        restack(parts[0], parts[1], ys, pl.ds(at, 256))
        return 0

    lax.fori_loop(0, HALF // 256, cotangent, 0)
    scatter(ys, backd, bk_s.at[1], bk_r.at[1], "expert", ex)

    order = (DOWN, GATE, UP)
    rs_step(DOWN, 2)
    rs_step(GATE, 3)
    rs_step(UP, 3)
    rs_step(DOWN, 1)
    rs_step(GATE, 2)
    rs_step(UP, 2)

    def collect(i, src, dst):
        def body(t, _):
            cols = pl.ds(pl.multiple_of(t * 256, 256), 256)
            for h in range(2):
                mo[i, :, pl.ds(pl.multiple_of(h * HALF + t * 256, 256), 256)] = nn(sel[i, h], src[:, cols]).astype(BF)
            return 0
        lax.fori_loop(0, HALF // 256, body, 0)
        cp = pltpu.make_async_copy(mo.at[i], dst, st.at[i])
        cp.start()
        return cp

    stores = []
    scatter_all(xs, backo, bk_s.at[0], bk_r.at[0], "expert").wait_recv()
    stores.append(collect(0, backo, out_hbm))
    rs_step(GATE, 1)
    rs_step(UP, 1)
    scatter_all(ys, backd, bk_s.at[1], bk_r.at[1], "expert").wait_recv()
    stores.append(collect(1, backd, dx_hbm))
    for i in order:
        rs_step(i, 0)
        cp = pltpu.make_async_copy(gr.at[i], (gg_hbm, gu_hbm, gd_hbm)[i].at[0], st.at[2 + i])
        cp.start()
        stores.append(cp)

    scatter_all(s2x, rcx, ex_s.at[0], ex_r.at[0], "expert").wait_send()
    scatter_all(s2y, rcy, ex_s.at[1], ex_r.at[1], "expert").wait_send()
    scatter_all(xs, backo, bk_s.at[0], bk_r.at[0], "expert").wait_send()
    scatter_all(ys, backd, bk_s.at[1], bk_r.at[1], "expert").wait_send()
    for g in gifts:
        g.wait_send()
    for i in range(3):
        shared_all(i).wait_send()
        for way in range(2):
            for hop in range(1, 5):
                ag(i, way, hop).wait_send()
                rs(i, way, hop).wait_send()
    for cp in stores:
        cp.wait()


def local(attn_rows, out_grad, owner_rows, routes, gates, gate_weight, up_weight, down_weight):
    any_ = pl.BlockSpec(memory_space=pl.ANY)
    vm = pl.BlockSpec(memory_space=pltpu.VMEM)
    V, S = pltpu.VMEM, pltpu.SemaphoreType.DMA
    rows_t = V((STK, HALF), BF)
    scratch = [rows_t] * 12 + [
        V((3, D, FF), BF), V((STK, STK), BF), V((STK, STK), BF), V((3, STK, 2 * TOK), BF), V((2, 2, TOK, STK), BF),
        V((Z, SH, STK), BF), V((Z, SH, STK), BF), V((Z, SH, ROWS), BF), V((Z, SH, ROWS), BF),
        V((STK, FF), BF), V((STK, FF), BF), V((STK, FF), BF), V((ROWS, FF), F32), V((ROWS, FF), F32),
        V((SH, FF), F32), V((3, SH, FF), BF), V((3, 2, 4, SH, FF), BF), V((2, TOK, D), BF), V((3, SH, FF), F32),
        S((7,)), S((2,)), S((2,)), S((2,)), S((2,)), S((2,)), S((2,)), S((3, 2, 4)), S((3, 2, 4)), S((3,)), S((3,)),
        S((5,)), S((5,)), S((3, 2, 4)), S((3, 2, 4)), S((5,)),
    ]
    grad = jax.ShapeDtypeStruct((1, SH, FF), F32)
    rows_o = jax.ShapeDtypeStruct((TOK, D), BF)
    return pl.pallas_call(
        kernel,
        out_shape=(rows_o, rows_o, grad, grad, grad),
        in_specs=[any_, any_, pl.BlockSpec(memory_space=pltpu.SMEM), vm, vm, any_, any_, any_],
        out_specs=(any_,) * 5,
        scratch_shapes=scratch,
        compiler_params=pltpu.CompilerParams(collective_id=0, has_side_effects=True, vmem_limit_bytes=63 << 20),
        cost_estimate=pl.CostEstimate(flops=20_000_000_000, bytes_accessed=12_000_000, transcendentals=300_000),
    )(attn_rows, out_grad, owner_rows, routes.reshape(1, TOK), gates.reshape(1, TOK),
      gate_weight, up_weight, down_weight)


def solution(mesh):
    in_specs = (
        P(("dp", "expert"), None),
        P(("dp", "expert"), None),
        P("expert", None),
        P(("dp", "expert"), None),
        P(("dp", "expert")),
        P("expert", "dp", None),
        P("expert", "dp", None),
        P("expert", "dp", None),
    )
    out_specs = (
        P(("dp", "expert"), None),
        P(("dp", "expert"), None),
        P("expert", "dp", None),
        P("expert", "dp", None),
        P("expert", "dp", None),
    )
    return jax.shard_map(local, mesh=mesh, in_specs=in_specs, out_specs=out_specs, check_vma=False)
```

```python
import jax
import jax.numpy as jnp
from jax import lax
from jax.experimental import pallas as pl
from jax.experimental.pallas import tpu as pltpu
from jax.sharding import PartitionSpec as P

MESH = pl.DeviceIdType.MESH
BF = jnp.bfloat16
F32 = jnp.float32
N = 16
Z = 8
CAP = 24
CH = 2 * CAP
HALF = 1024
ROWS = N * CAP
STK = 2 * ROWS
TOK = 256
D = 2048
FF = 768
SH = 128
GATE, UP, DOWN = 0, 1, 2
PLANE = ((2, 2), (1, 3), (3, 1), (1, 1), (3, 3), (2, 1), (1, 2), (2, 3), (3, 2), (2, 0), (0, 2), (1, 0), (0, 1), (3, 0), (0, 3))


def nn(a, b):
    return jnp.dot(a, b, preferred_element_type=F32)


def nt(a, b):
    return lax.dot_general(a, b, (((1,), (1,)), ((), ())), preferred_element_type=F32)


def kernel(
    x_hbm, dy_hbm, lens, routes, gates, wg_hbm, wu_hbm, wd_hbm,
    out_hbm, dx_hbm, gg_hbm, gu_hbm, gd_hbm,
    xin, yin, xs, ys, gotx, goty, s2x, s2y, rcx, rcy, backo, backd,
    w, perm, perm_g, a_t, sel,
    xt, yt, xt_s, yt_s, hid, gcot, ucot, f1, f2, tmp, s4, sb, mo, gr,
    ld, rel_s, rel_r, ex_s, ex_r, bk_s, bk_r, ag_s, ag_r, sib_s, sib_r, act_s, act_r, rs_s, rs_r, st,
):
    dp = lax.axis_index("dp")
    ex = lax.axis_index("expert")
    z = dp // 2
    c = lax.rem(dp, 2)
    sibling = {"dp": dp + 1 - 2 * c}

    loads = []
    for i, (src, dst) in enumerate(((x_hbm, xin), (dy_hbm, yin))):
        for h in range(2):
            loads.append(pltpu.make_async_copy(
                src.at[:, pl.ds(h * HALF, HALF)], dst.at[pl.ds(h * ROWS, ROWS)], ld.at[2 * i + h]))
    my_rows = pl.multiple_of(dp * SH, SH)
    for i, src in enumerate((wg_hbm, wu_hbm, wd_hbm)):
        loads.append(pltpu.make_async_copy(src.at[0], w.at[i, pl.ds(my_rows, SH)], ld.at[4 + i]))
    for cp in loads:
        cp.start()

    bar = pltpu.get_barrier_semaphore()

    def greet(i, _):
        pl.semaphore_signal(bar, 1, device_id={"dp": lax.rem(dp + i, N)}, device_id_type=MESH)
        pl.semaphore_signal(bar, 1, device_id={"expert": lax.rem(ex + i, N)}, device_id_type=MESH)
        return 0

    lax.fori_loop(1, N, greet, 0)

    def prefix(i, acc):
        return acc + jnp.where(i < dp, lens[0, i], 0)

    start = lax.fori_loop(0, N, prefix, jnp.int32(0))
    col = lax.broadcasted_iota(jnp.int32, (1, STK), 1)
    right_half = (col >= ROWS).astype(jnp.int32)
    r = col - ROWS * right_half
    dest = ((r + start) & (N - 1)) * CH + CAP * right_half + (r >> 4)
    row_iota = lax.broadcasted_iota(jnp.int32, (STK, STK), 0)
    perm[...] = jnp.where(row_iota == dest, 1.0, 0.0).astype(BF)

    def permute(p_ref, src, dst):
        def body(t, _):
            cols = pl.ds(pl.multiple_of(t * 256, 256), 256)
            dst[:, cols] = nn(p_ref[...], src[:, cols]).astype(BF)
            return 0
        lax.fori_loop(0, HALF // 256, body, 0)

    def tile(i):
        return pl.ds(pl.multiple_of(i * CH, CH), CH)

    def scatter(src, dst, ssem, rsem, axis, me):
        def body(i, _):
            t = lax.rem(me + i, N)
            pltpu.make_async_remote_copy(
                src_ref=src.at[tile(t)], dst_ref=dst.at[tile(me)], send_sem=ssem, recv_sem=rsem,
                device_id={axis: t}, device_id_type=MESH).start()
            return 0
        lax.fori_loop(1, N, body, 0)
        dst[tile(me), :] = src[tile(me), :]

    def spread(src, dst, ssem, rsem):
        row, column = ex // 4, lax.rem(ex, 4)
        for a, b in PLANE:
            t = lax.rem(row + a, 4) * 4 + lax.rem(column + b, 4)
            pltpu.make_async_remote_copy(
                src_ref=src.at[tile(t)], dst_ref=dst.at[tile(ex)], send_sem=ssem, recv_sem=rsem,
                device_id={"expert": t}, device_id_type=MESH).start()
        dst[tile(ex), :] = src[tile(ex), :]

    def scatter_all(src, dst, ssem, rsem, axis):
        me = dp if axis == "dp" else ex
        span = pl.ds(0, (N - 1) * CH)
        return pltpu.make_async_remote_copy(
            src_ref=src.at[span], dst_ref=dst.at[span], send_sem=ssem, recv_sem=rsem,
            device_id={axis: lax.rem(me + 1, N)}, device_id_type=MESH)

    def shard(o, lo=0, n=SH):
        return pl.ds(pl.multiple_of((2 * o + c) * SH + lo, 64), n)

    def span_of(hop, way):
        if hop < 4:
            return 0, SH
        return (0 if way == 0 else 64), 64

    def chip(k):
        return lax.rem(z + k + 2 * Z, Z)

    def ag(i, way, hop):
        sign = 1 - 2 * way
        lo, n = span_of(hop, way)
        rows = shard(chip(-sign * (hop - 1)), lo, n)
        return pltpu.make_async_remote_copy(
            src_ref=w.at[i, rows], dst_ref=w.at[i, rows], send_sem=ag_s.at[i, way, hop - 1],
            recv_sem=ag_r.at[i, way, hop - 1], device_id={"dp": 2 * chip(sign) + c}, device_id_type=MESH)

    def ag_in(i, way, hop):
        sign = 1 - 2 * way
        lo, n = span_of(hop, way)
        rows = shard(chip(-sign * hop), lo, n)
        return pltpu.make_async_remote_copy(
            src_ref=w.at[i, rows], dst_ref=w.at[i, rows], send_sem=ag_s.at[i, way, hop - 1],
            recv_sem=ag_r.at[i, way, hop - 1], device_id={"dp": 2 * chip(sign) + c}, device_id_type=MESH)

    def share(i, o):
        rows = shard(o)
        return pltpu.make_async_remote_copy(
            src_ref=w.at[i, rows], dst_ref=w.at[i, rows], send_sem=sib_s.at[i], recv_sem=sib_r.at[i],
            device_id=sibling, device_id_type=MESH)

    def shared_all(i):
        rows = pl.ds(0, Z * SH)
        return pltpu.make_async_remote_copy(
            src_ref=w.at[i, rows], dst_ref=w.at[i, rows], send_sem=sib_s.at[i], recv_sem=sib_r.at[i],
            device_id=sibling, device_id_type=MESH)

    def ag_step(i, hop):
        for way in range(2):
            ag_in(i, way, hop).wait_recv()
            if hop < 4:
                ag(i, way, hop + 1).start()
                share(i, chip((2 * way - 1) * hop)).start()
        if hop == 4:
            share(i, chip(4)).start()

    for i in range(3):
        loads[4 + i].wait()
    pl.semaphore_wait(bar, 2 * (N - 1))

    def ag_first(i):
        ag(i, 0, 1).start()
        ag(i, 1, 1).start()
        share(i, z).start()

    ag_first(GATE)
    ag_first(UP)
    loads[0].wait()
    loads[1].wait()
    permute(perm, xin, xs)
    scatter(xs, gotx, rel_s.at[0], rel_r.at[0], "dp", dp)
    loads[2].wait()
    loads[3].wait()
    permute(perm, yin, ys)
    scatter(ys, goty, rel_s.at[1], rel_r.at[1], "dp", dp)
    ag_first(DOWN)

    expert_iota = lax.broadcasted_iota(jnp.int32, (N, TOK), 0)
    route = routes[...]
    hot = expert_iota == route
    hot_f = jnp.where(hot, 1.0, 0.0)
    earlier = (lax.broadcasted_iota(jnp.int32, (TOK, TOK), 0) < lax.broadcasted_iota(jnp.int32, (TOK, TOK), 1))
    before = nn(hot_f.astype(BF), jnp.where(earlier, 1.0, 0.0).astype(BF))
    rank = jnp.sum(before * hot_f, axis=0, keepdims=True).astype(jnp.int32)
    slot = route * CH + rank
    pos = N * lax.broadcasted_iota(jnp.int32, (1, TOK), 1) + dp
    owner = jnp.zeros((1, TOK), jnp.int32)
    first = jnp.zeros((1, TOK), jnp.int32)
    end = jnp.int32(0)
    for b in range(N):
        end = end + lens[0, b]
        past = pos >= end
        owner = owner + jnp.where(past, 1, 0)
        first = jnp.where(past, end, first)
    got_row = owner * CH + ((pos - first) >> 4)
    gate_f = gates[...].astype(F32)
    tall = lax.broadcasted_iota(jnp.int32, (STK, TOK), 0)
    eye = jnp.where(
        lax.broadcasted_iota(jnp.int32, (TOK, TOK), 0) == lax.broadcasted_iota(jnp.int32, (TOK, TOK), 1), 1.0, 0.0
    ).astype(BF)
    for h in range(2):
        cols = pl.ds(h * TOK, TOK)
        hit = tall == slot + h * CAP
        plain = jnp.where(hit, 1.0, 0.0).astype(BF)
        gated = jnp.where(hit, gate_f, 0.0).astype(BF)
        a_t[0, :, cols] = plain
        a_t[1, :, cols] = gated
        a_t[2, :, cols] = jnp.where(tall == got_row + h * CAP, 1.0, 0.0).astype(BF)
        sel[0, h] = nt(eye, gated).astype(BF)
        sel[1, h] = nt(eye, plain).astype(BF)

    def build(t, _):
        rows = pl.ds(pl.multiple_of(t * 256, 256), 256)
        perm[rows, :] = nt(a_t[0, rows, :], a_t[2]).astype(BF)
        perm_g[rows, :] = nt(a_t[1, rows, :], a_t[2]).astype(BF)
        return 0

    lax.fori_loop(0, STK // 256, build, 0)

    def unstack(src, dst):
        def body(t, _):
            one = src[tile(2 * t), :].astype(F32)
            two = src[tile(2 * t + 1), :].astype(F32)
            at = pl.multiple_of(t * CH, CH)
            dst[pl.ds(at, CH), :] = jnp.concatenate([one[:CAP], two[:CAP]], axis=0).astype(BF)
            dst[pl.ds(at + ROWS, CH), :] = jnp.concatenate([one[CAP:], two[CAP:]], axis=0).astype(BF)
            return 0
        lax.fori_loop(0, N // 2, body, 0)

    own_rows = pl.ds(pl.multiple_of(c * ROWS, ROWS), ROWS)
    eye_s = eye[:SH, :SH]

    def turn(src, mine, theirs):
        def body(t, _):
            for par, dst in ((c, None), (1 - c, theirs)):
                d = 2 * t + par
                block = src[pl.ds(pl.multiple_of((d // Z) * ROWS, ROWS), ROWS),
                            pl.ds(pl.multiple_of(lax.rem(d, Z) * SH, SH), SH)]
                turned = nt(eye_s, block).astype(BF)
                if dst is None:
                    mine[t, :, own_rows] = turned
                else:
                    dst[t] = turned
            return 0
        lax.fori_loop(0, Z, body, 0)

    def give(i, src, dst):
        return pltpu.make_async_remote_copy(
            src_ref=src, dst_ref=dst, send_sem=act_s.at[i], recv_sem=act_r.at[i],
            device_id=sibling, device_id_type=MESH)

    gifts = (
        give(0, xt_s, xt.at[:, :, own_rows]),
        give(1, yt_s, yt.at[:, :, own_rows]),
        give(2, hid.at[own_rows], hid.at[own_rows]),
        give(3, gcot.at[own_rows], gcot.at[own_rows]),
        give(4, ucot.at[own_rows], ucot.at[own_rows]),
    )

    ag_step(GATE, 1)
    ag_step(UP, 1)
    scatter_all(xs, gotx, rel_s.at[0], rel_r.at[0], "dp").wait_recv()
    permute(perm, gotx, s2x)
    spread(s2x, rcx, ex_s.at[0], ex_r.at[0])
    scatter_all(ys, goty, rel_s.at[1], rel_r.at[1], "dp").wait_recv()
    permute(perm_g, goty, s2y)
    spread(s2y, rcy, ex_s.at[1], ex_r.at[1])
    ag_step(GATE, 2)
    scatter_all(s2x, rcx, ex_s.at[0], ex_r.at[0], "expert").wait_recv()
    unstack(rcx, xin)
    turn(xin, xt, xt_s)
    gifts[0].start()
    ag_step(UP, 2)
    ag_step(DOWN, 1)
    ag_step(GATE, 3)
    ag_step(UP, 3)
    scatter_all(s2y, rcy, ex_s.at[1], ex_r.at[1], "expert").wait_recv()
    unstack(rcy, yin)
    turn(yin, yt, yt_s)
    gifts[1].start()
    ag_step(DOWN, 2)
    ag_step(GATE, 4)
    ag_step(UP, 4)
    shared_all(GATE).wait_recv()
    shared_all(UP).wait_recv()

    def forward(t, _):
        cols = pl.ds(pl.multiple_of(t * 256, 256), 256)
        g = nn(xin[:ROWS, :], w[GATE, :HALF, cols]) + nn(xin[ROWS:, :], w[GATE, HALF:, cols])
        u = nn(xin[:ROWS, :], w[UP, :HALF, cols]) + nn(xin[ROWS:, :], w[UP, HALF:, cols])
        sg = jax.nn.sigmoid(g)
        active = g * sg
        hid[own_rows, cols] = (active * u).astype(BF)
        f1[:, cols] = u * sg * (1.0 + g * (1.0 - sg))
        f2[:, cols] = active
        return 0

    lax.fori_loop(0, 2, forward, 0)
    lax.fori_loop(2, FF // 256, forward, 0)
    gifts[2].start()
    ag_step(DOWN, 3)

    def rs(i, way, hop):
        sign = 1 - 2 * way
        lo, n = span_of(hop, way)
        rows = pl.ds(lo, n)
        src = s4.at[i, rows] if hop == 4 else sb.at[i, way, hop, rows]
        return pltpu.make_async_remote_copy(
            src_ref=src, dst_ref=sb.at[i, way, hop - 1, rows], send_sem=rs_s.at[i, way, hop - 1],
            recv_sem=rs_r.at[i, way, hop - 1], device_id={"dp": 2 * chip(sign) + c}, device_id_type=MESH)

    def term(i, k):
        left = yt if i == DOWN else xt
        right = (gcot, ucot, hid)[i]
        return nn(left[chip(k)], right[...])

    def rs_step(i, hop):
        if hop == 4:
            s4[i] = term(i, 4).astype(BF)
            rs(i, 0, 4).start()
            rs(i, 1, 4).start()
            return
        if hop == 0:
            tmp[...] = term(i, 0)
            for way in range(2):
                rs(i, way, 1).wait_recv()
            gr[i] = tmp[...] + sb[i, 0, 0].astype(F32) + sb[i, 1, 0].astype(F32)
            return
        for way in range(2):
            tmp[...] = term(i, (1 - 2 * way) * hop)
            rs(i, way, hop + 1).wait_recv()
            lo, n = span_of(hop + 1, way)
            sb[i, way, hop, pl.ds(lo, n)] = (
                tmp[pl.ds(lo, n)] + sb[i, way, hop, pl.ds(lo, n)].astype(F32)).astype(BF)
            if n < SH:
                sb[i, way, hop, pl.ds(64 - lo, 64)] = tmp[pl.ds(64 - lo, 64)].astype(BF)
            rs(i, way, hop).start()

    gifts[1].wait_recv()
    gifts[2].wait_recv()
    rs_step(DOWN, 4)
    ag_step(DOWN, 4)
    shared_all(DOWN).wait_recv()

    def backward(t, _):
        cols = pl.ds(pl.multiple_of(t * 256, 256), 256)
        hc = nn(yin[:ROWS, :], w[DOWN, :HALF, cols]) + nn(yin[ROWS:, :], w[DOWN, HALF:, cols])
        gcot[own_rows, cols] = (hc * f1[:, cols]).astype(BF)
        ucot[own_rows, cols] = (hc * f2[:, cols]).astype(BF)
        return 0

    lax.fori_loop(0, FF // 256, backward, 0)
    gifts[3].start()
    gifts[4].start()
    rs_step(DOWN, 3)

    def restack(first, second, dst, cols):
        for e in range(N):
            rows = slice(e * CAP, (e + 1) * CAP)
            dst[pl.ds(e * CH, CH), cols] = jnp.concatenate([first[rows], second[rows]], axis=0).astype(BF)

    scatter_all(xs, gotx, rel_s.at[0], rel_r.at[0], "dp").wait_send()
    scatter_all(ys, goty, rel_s.at[1], rel_r.at[1], "dp").wait_send()

    def produce(t, _):
        at = pl.multiple_of(t * 256, 256)
        left = hid[own_rows, :]
        restack(nt(left, w[DOWN, pl.ds(at, 256), :]), nt(left, w[DOWN, pl.ds(at + HALF, 256), :]),
                xs, pl.ds(at, 256))
        return 0

    lax.fori_loop(0, HALF // 256, produce, 0)
    spread(xs, backo, bk_s.at[0], bk_r.at[0])
    gifts[0].wait_recv()
    gifts[3].wait_recv()
    rs_step(GATE, 4)
    gifts[4].wait_recv()
    rs_step(UP, 4)

    def cotangent(t, _):
        at = pl.multiple_of(t * 256, 256)
        lg, lu = gcot[own_rows, :], ucot[own_rows, :]
        parts = []
        for h in range(2):
            rows = pl.ds(at + h * HALF, 256)
            parts.append(nt(lg, w[GATE, rows, :]) + nt(lu, w[UP, rows, :]))
        restack(parts[0], parts[1], ys, pl.ds(at, 256))
        return 0

    lax.fori_loop(0, HALF // 256, cotangent, 0)
    spread(ys, backd, bk_s.at[1], bk_r.at[1])

    order = (DOWN, GATE, UP)
    rs_step(DOWN, 2)
    rs_step(GATE, 3)
    rs_step(UP, 3)
    rs_step(DOWN, 1)
    rs_step(GATE, 2)
    rs_step(UP, 2)

    def collect(i, src, dst):
        def body(t, _):
            cols = pl.ds(pl.multiple_of(t * 256, 256), 256)
            for h in range(2):
                mo[i, :, pl.ds(pl.multiple_of(h * HALF + t * 256, 256), 256)] = nn(sel[i, h], src[:, cols]).astype(BF)
            return 0
        lax.fori_loop(0, HALF // 256, body, 0)
        cp = pltpu.make_async_copy(mo.at[i], dst, st.at[i])
        cp.start()
        return cp

    stores = []
    scatter_all(xs, backo, bk_s.at[0], bk_r.at[0], "expert").wait_recv()
    stores.append(collect(0, backo, out_hbm))
    rs_step(GATE, 1)
    rs_step(UP, 1)
    scatter_all(ys, backd, bk_s.at[1], bk_r.at[1], "expert").wait_recv()
    stores.append(collect(1, backd, dx_hbm))
    for i in order:
        rs_step(i, 0)
        cp = pltpu.make_async_copy(gr.at[i], (gg_hbm, gu_hbm, gd_hbm)[i].at[0], st.at[2 + i])
        cp.start()
        stores.append(cp)

    scatter_all(s2x, rcx, ex_s.at[0], ex_r.at[0], "expert").wait_send()
    scatter_all(s2y, rcy, ex_s.at[1], ex_r.at[1], "expert").wait_send()
    scatter_all(xs, backo, bk_s.at[0], bk_r.at[0], "expert").wait_send()
    scatter_all(ys, backd, bk_s.at[1], bk_r.at[1], "expert").wait_send()
    for g in gifts:
        g.wait_send()
    for i in range(3):
        shared_all(i).wait_send()
        for way in range(2):
            for hop in range(1, 5):
                ag(i, way, hop).wait_send()
                rs(i, way, hop).wait_send()
    for cp in stores:
        cp.wait()


def hand_over(*refs):
    src, dst, held, sems = refs[:5], refs[5:10], refs[10:15], refs[15]
    reads = [pltpu.make_async_copy(src[i], held[i], sems.at[0, i]) for i in range(5)]
    writes = [pltpu.make_async_copy(held[i], dst[i], sems.at[1, i]) for i in range(5)]
    for cp in reads:
        cp.start()
    for i in range(5):
        reads[i].wait()
        writes[i].start()
    for cp in writes:
        cp.wait()


def local(attn_rows, out_grad, owner_rows, routes, gates, gate_weight, up_weight, down_weight):
    any_ = pl.BlockSpec(memory_space=pl.ANY)
    vm = pl.BlockSpec(memory_space=pltpu.VMEM)
    V, S = pltpu.VMEM, pltpu.SemaphoreType.DMA
    rows_t = V((STK, HALF), BF)
    scratch = [rows_t] * 12 + [
        V((3, D, FF), BF), V((STK, STK), BF), V((STK, STK), BF), V((3, STK, 2 * TOK), BF), V((2, 2, TOK, STK), BF),
        V((Z, SH, STK), BF), V((Z, SH, STK), BF), V((Z, SH, ROWS), BF), V((Z, SH, ROWS), BF),
        V((STK, FF), BF), V((STK, FF), BF), V((STK, FF), BF), V((ROWS, FF), F32), V((ROWS, FF), F32),
        V((SH, FF), F32), V((3, SH, FF), BF), V((3, 2, 4, SH, FF), BF), V((2, TOK, D), BF), V((3, SH, FF), F32),
        S((7,)), S((2,)), S((2,)), S((2,)), S((2,)), S((2,)), S((2,)), S((3, 2, 4)), S((3, 2, 4)), S((3,)), S((3,)),
        S((5,)), S((5,)), S((3, 2, 4)), S((3, 2, 4)), S((5,)),
    ]
    grad = jax.ShapeDtypeStruct((1, SH, FF), F32)
    rows_o = jax.ShapeDtypeStruct((TOK, D), BF)
    results = pl.pallas_call(
        kernel,
        out_shape=(rows_o, rows_o, grad, grad, grad),
        in_specs=[any_, any_, pl.BlockSpec(memory_space=pltpu.SMEM), vm, vm, any_, any_, any_],
        out_specs=(any_,) * 5,
        scratch_shapes=scratch,
        compiler_params=pltpu.CompilerParams(collective_id=0, has_side_effects=True, vmem_limit_bytes=63 << 20),
        cost_estimate=pl.CostEstimate(flops=20_000_000_000, bytes_accessed=12_000_000, transcendentals=300_000),
    )(attn_rows, out_grad, owner_rows, routes.reshape(1, TOK), gates.reshape(1, TOK),
      gate_weight, up_weight, down_weight)
    return pl.pallas_call(
        hand_over,
        out_shape=(rows_o, rows_o, grad, grad, grad),
        in_specs=[any_] * 5,
        out_specs=(any_,) * 5,
        scratch_shapes=[V((TOK, D), BF), V((TOK, D), BF)] + [V((1, SH, FF), F32)] * 3 + [S((2, 5))],
    )(*results)


def solution(mesh):
    in_specs = (
        P(("dp", "expert"), None),
        P(("dp", "expert"), None),
        P("expert", None),
        P(("dp", "expert"), None),
        P(("dp", "expert")),
        P("expert", "dp", None),
        P("expert", "dp", None),
        P("expert", "dp", None),
    )
    out_specs = (
        P(("dp", "expert"), None),
        P(("dp", "expert"), None),
        P("expert", "dp", None),
        P("expert", "dp", None),
        P("expert", "dp", None),
    )
    return jax.shard_map(local, mesh=mesh, in_specs=in_specs, out_specs=out_specs, check_vma=False)
```

```python
import jax
import jax.numpy as jnp
from jax import lax
from jax.experimental import pallas as pl
from jax.experimental.pallas import tpu as pltpu
from jax.sharding import PartitionSpec as P

MESH = pl.DeviceIdType.MESH
BF = jnp.bfloat16
F32 = jnp.float32
N = 16
Z = 8
CAP = 24
CH = 2 * CAP
HALF = 1024
ROWS = N * CAP
STK = 2 * ROWS
TOK = 256
D = 2048
FF = 768
SH = 128
GATE, UP, DOWN = 0, 1, 2
PLANE = ((2, 2), (1, 3), (3, 1), (1, 1), (3, 3), (2, 1), (1, 2), (2, 3), (3, 2), (2, 0), (0, 2), (1, 0), (0, 1), (3, 0), (0, 3))


def nn(a, b):
    return jnp.dot(a, b, preferred_element_type=F32)


def nt(a, b):
    return lax.dot_general(a, b, (((1,), (1,)), ((), ())), preferred_element_type=F32)


def kernel(
    x_hbm, dy_hbm, lens, routes, gates, wg_hbm, wu_hbm, wd_hbm,
    out_hbm, dx_hbm, gg_hbm, gu_hbm, gd_hbm,
    xin, yin, xs, ys, gotx, goty, s2x, s2y, rcx, rcy, backo, backd,
    w, perm, perm_g, a_t, sel,
    xt, yt, xt_s, yt_s, hid, gcot, ucot, f1, f2, f3, tmp, s4, sb, mo, gr,
    ld, rel_s, rel_r, ex_s, ex_r, bk_s, bk_r, ag_s, ag_r, sib_s, sib_r, act_s, act_r, rs_s, rs_r, st,
):
    dp = lax.axis_index("dp")
    ex = lax.axis_index("expert")
    z = dp // 2
    c = lax.rem(dp, 2)
    sibling = {"dp": dp + 1 - 2 * c}

    loads = []
    for i, (src, dst) in enumerate(((x_hbm, xin), (dy_hbm, yin))):
        for h in range(2):
            loads.append(pltpu.make_async_copy(
                src.at[:, pl.ds(h * HALF, HALF)], dst.at[pl.ds(h * ROWS, ROWS)], ld.at[2 * i + h]))
    my_half = pl.ds(pl.multiple_of(c * SH, SH), SH)
    for i, src in enumerate((wg_hbm, wu_hbm, wd_hbm)):
        loads.append(pltpu.make_async_copy(src.at[0], w.at[i, 0, my_half], ld.at[4 + i]))
    for cp in loads:
        cp.start()

    bar = pltpu.get_barrier_semaphore()

    def greet(i, _):
        pl.semaphore_signal(bar, 1, device_id={"dp": lax.rem(dp + i, N)}, device_id_type=MESH)
        pl.semaphore_signal(bar, 1, device_id={"expert": lax.rem(ex + i, N)}, device_id_type=MESH)
        return 0

    lax.fori_loop(1, N, greet, 0)

    def permute(p_ref, src, dst):
        def body(t, _):
            cols = pl.ds(pl.multiple_of(t * 256, 256), 256)
            dst[:, cols] = nn(p_ref[...], src[:, cols]).astype(BF)
            return 0
        lax.fori_loop(0, HALF // 256, body, 0)

    def tile(i):
        return pl.ds(pl.multiple_of(i * CH, CH), CH)

    def scatter(src, dst, ssem, rsem, axis, me):
        def body(i, _):
            t = lax.rem(me + i, N)
            pltpu.make_async_remote_copy(
                src_ref=src.at[tile(t)], dst_ref=dst.at[tile(me)], send_sem=ssem, recv_sem=rsem,
                device_id={axis: t}, device_id_type=MESH).start()
            return 0
        lax.fori_loop(1, N, body, 0)
        dst[tile(me), :] = src[tile(me), :]

    def spread(src, dst, ssem, rsem):
        row, column = ex // 4, lax.rem(ex, 4)
        for a, b in PLANE:
            t = lax.rem(row + a, 4) * 4 + lax.rem(column + b, 4)
            pltpu.make_async_remote_copy(
                src_ref=src.at[tile(t)], dst_ref=dst.at[tile(ex)], send_sem=ssem, recv_sem=rsem,
                device_id={"expert": t}, device_id_type=MESH).start()
        dst[tile(ex), :] = src[tile(ex), :]

    def scatter_all(src, dst, ssem, rsem, axis):
        me = dp if axis == "dp" else ex
        span = pl.ds(0, (N - 1) * CH)
        return pltpu.make_async_remote_copy(
            src_ref=src.at[span], dst_ref=dst.at[span], send_sem=ssem, recv_sem=rsem,
            device_id={axis: lax.rem(me + 1, N)}, device_id_type=MESH)

    def span_of(hop, way):
        if hop < 4:
            return 0, SH
        return (0 if way == 0 else 64), 64

    def chip(k):
        return lax.rem(z + k + 2 * Z, Z)

    def ag(i, way, hop):
        sign = 1 - 2 * way
        lo, n = span_of(hop, way)
        rows = pl.ds(pl.multiple_of(c * SH + lo, 64), n)
        return pltpu.make_async_remote_copy(
            src_ref=w.at[i, (-sign * (hop - 1)) % Z, rows], dst_ref=w.at[i, (-sign * hop) % Z, rows],
            send_sem=ag_s.at[i, way, hop - 1], recv_sem=ag_r.at[i, way, hop - 1],
            device_id={"dp": 2 * chip(sign) + c}, device_id_type=MESH)

    def share(i, k, hop):
        block = w.at[i, k % Z, my_half]
        return pltpu.make_async_remote_copy(
            src_ref=block, dst_ref=block, send_sem=sib_s.at[i, hop], recv_sem=sib_r.at[i, hop],
            device_id=sibling, device_id_type=MESH)

    def shared(i, hop):
        block = w.at[i, hop, pl.ds(0, SH if hop in (0, 4) else 2 * SH)]
        return pltpu.make_async_remote_copy(
            src_ref=block, dst_ref=block, send_sem=sib_s.at[i, hop], recv_sem=sib_r.at[i, hop],
            device_id=sibling, device_id_type=MESH)

    def ag_step(i, hop):
        for way in range(2):
            ag(i, way, hop).wait_recv()
            if hop < 4:
                ag(i, way, hop + 1).start()
                share(i, (2 * way - 1) * hop, hop).start()
        if hop == 4:
            share(i, 4, 4).start()

    for i in range(3):
        loads[4 + i].wait()
    pl.semaphore_wait(bar, 2 * (N - 1))

    def ag_first(i):
        ag(i, 0, 1).start()
        ag(i, 1, 1).start()
        share(i, 0, 0).start()

    ag_first(GATE)
    ag_first(UP)
    def prefix(i, acc):
        return acc + jnp.where(i < dp, lens[0, i], 0)

    start = lax.fori_loop(0, N, prefix, jnp.int32(0))
    col = lax.broadcasted_iota(jnp.int32, (1, STK), 1)
    right_half = (col >= ROWS).astype(jnp.int32)
    r = col - ROWS * right_half
    dest = ((r + start) & (N - 1)) * CH + CAP * right_half + (r >> 4)
    row_iota = lax.broadcasted_iota(jnp.int32, (STK, STK), 0)
    perm[...] = jnp.where(row_iota == dest, 1.0, 0.0).astype(BF)

    loads[0].wait()
    loads[1].wait()
    permute(perm, xin, xs)
    scatter(xs, gotx, rel_s.at[0], rel_r.at[0], "dp", dp)
    loads[2].wait()
    loads[3].wait()
    permute(perm, yin, ys)
    scatter(ys, goty, rel_s.at[1], rel_r.at[1], "dp", dp)
    ag_first(DOWN)

    expert_iota = lax.broadcasted_iota(jnp.int32, (N, TOK), 0)
    route = routes[...]
    hot = expert_iota == route
    hot_f = jnp.where(hot, 1.0, 0.0)
    earlier = (lax.broadcasted_iota(jnp.int32, (TOK, TOK), 0) < lax.broadcasted_iota(jnp.int32, (TOK, TOK), 1))
    before = nn(hot_f.astype(BF), jnp.where(earlier, 1.0, 0.0).astype(BF))
    rank = jnp.sum(before * hot_f, axis=0, keepdims=True).astype(jnp.int32)
    slot = route * CH + rank
    pos = N * lax.broadcasted_iota(jnp.int32, (1, TOK), 1) + dp
    owner = jnp.zeros((1, TOK), jnp.int32)
    first = jnp.zeros((1, TOK), jnp.int32)
    end = jnp.int32(0)
    for b in range(N):
        end = end + lens[0, b]
        past = pos >= end
        owner = owner + jnp.where(past, 1, 0)
        first = jnp.where(past, end, first)
    got_row = owner * CH + ((pos - first) >> 4)
    gate_f = gates[...].astype(F32)
    tall = lax.broadcasted_iota(jnp.int32, (STK, TOK), 0)
    eye = jnp.where(
        lax.broadcasted_iota(jnp.int32, (TOK, TOK), 0) == lax.broadcasted_iota(jnp.int32, (TOK, TOK), 1), 1.0, 0.0
    ).astype(BF)
    for h in range(2):
        cols = pl.ds(h * TOK, TOK)
        hit = tall == slot + h * CAP
        plain = jnp.where(hit, 1.0, 0.0).astype(BF)
        gated = jnp.where(hit, gate_f, 0.0).astype(BF)
        a_t[0, :, cols] = plain
        a_t[1, :, cols] = gated
        a_t[2, :, cols] = jnp.where(tall == got_row + h * CAP, 1.0, 0.0).astype(BF)
        sel[0, h] = nt(eye, gated).astype(BF)
        sel[1, h] = nt(eye, plain).astype(BF)

    def build(t, _):
        rows = pl.ds(pl.multiple_of(t * 256, 256), 256)
        perm[rows, :] = nt(a_t[0, rows, :], a_t[2]).astype(BF)
        perm_g[rows, :] = nt(a_t[1, rows, :], a_t[2]).astype(BF)
        return 0

    lax.fori_loop(0, STK // 256, build, 0)

    def unstack(src, dst):
        def body(t, _):
            one = src[tile(2 * t), :].astype(F32)
            two = src[tile(2 * t + 1), :].astype(F32)
            at = pl.multiple_of(t * CH, CH)
            dst[pl.ds(at, CH), :] = jnp.concatenate([one[:CAP], two[:CAP]], axis=0).astype(BF)
            dst[pl.ds(at + ROWS, CH), :] = jnp.concatenate([one[CAP:], two[CAP:]], axis=0).astype(BF)
            return 0
        lax.fori_loop(0, N // 2, body, 0)

    own_rows = pl.ds(pl.multiple_of(c * ROWS, ROWS), ROWS)
    eye_s = eye[:SH, :SH]

    def turn(src, mine, theirs):
        def body(t, _):
            for par, dst in ((c, None), (1 - c, theirs)):
                d = 2 * t + par
                block = src[pl.ds(pl.multiple_of((d // Z) * ROWS, ROWS), ROWS),
                            pl.ds(pl.multiple_of(lax.rem(d, Z) * SH, SH), SH)]
                turned = nt(eye_s, block).astype(BF)
                if dst is None:
                    mine[t, :, own_rows] = turned
                else:
                    dst[t] = turned
            return 0
        lax.fori_loop(0, Z, body, 0)

    def give(i, src, dst):
        return pltpu.make_async_remote_copy(
            src_ref=src, dst_ref=dst, send_sem=act_s.at[i], recv_sem=act_r.at[i],
            device_id=sibling, device_id_type=MESH)

    gifts = (
        give(0, xt_s, xt.at[:, :, own_rows]),
        give(1, yt_s, yt.at[:, :, own_rows]),
        give(2, hid.at[own_rows], hid.at[own_rows]),
        give(3, gcot.at[own_rows], gcot.at[own_rows]),
        give(4, ucot.at[own_rows], ucot.at[own_rows]),
    )

    ag_step(GATE, 1)
    ag_step(UP, 1)
    scatter_all(xs, gotx, rel_s.at[0], rel_r.at[0], "dp").wait_recv()
    permute(perm, gotx, s2x)
    spread(s2x, rcx, ex_s.at[0], ex_r.at[0])
    scatter_all(ys, goty, rel_s.at[1], rel_r.at[1], "dp").wait_recv()
    permute(perm_g, goty, s2y)
    spread(s2y, rcy, ex_s.at[1], ex_r.at[1])
    ag_step(GATE, 2)
    scatter_all(s2x, rcx, ex_s.at[0], ex_r.at[0], "expert").wait_recv()
    unstack(rcx, xin)
    turn(xin, xt, xt_s)
    gifts[0].start()
    ag_step(UP, 2)
    ag_step(DOWN, 1)

    def chip_product(src, i, k, cols):
        o = chip(k)
        rows = src[pl.ds(pl.multiple_of((o // 4) * ROWS, ROWS), ROWS), pl.ds(pl.multiple_of(lax.rem(o, 4) * 256, 256), 256)]
        return nn(rows, w[i, k % Z, :, cols])

    def part(i, src, acc, hops):
        steps = []
        for hop in hops:
            shared(i, hop).wait_recv()
            steps += [hop] if hop in (0, 4) else [hop, -hop]
        for t in range(FF // 256):
            cols = pl.ds(t * 256, 256)
            total = chip_product(src, i, steps[0], cols)
            for k in steps[1:]:
                total = total + chip_product(src, i, k, cols)
            acc[:, cols] = total if 0 in hops else acc[:, cols] + total

    part(GATE, xin, f1, (0, 1))
    part(UP, xin, f2, (0, 1))
    ag_step(GATE, 3)
    part(GATE, xin, f1, (2,))
    part(UP, xin, f2, (2,))
    ag_step(UP, 3)
    scatter_all(s2y, rcy, ex_s.at[1], ex_r.at[1], "expert").wait_recv()
    unstack(rcy, yin)
    turn(yin, yt, yt_s)
    gifts[1].start()
    ag_step(DOWN, 2)
    part(GATE, xin, f1, (3,))
    part(UP, xin, f2, (3,))
    part(DOWN, yin, f3, (0, 1))
    ag_step(GATE, 4)
    ag_step(UP, 4)
    part(DOWN, yin, f3, (2,))
    shared(GATE, 4).wait_recv()
    shared(UP, 4).wait_recv()

    def forward(t, _):
        cols = pl.ds(pl.multiple_of(t * 256, 256), 256)
        g = f1[:, cols] + chip_product(xin, GATE, 4, cols)
        u = f2[:, cols] + chip_product(xin, UP, 4, cols)
        sg = jax.nn.sigmoid(g)
        active = g * sg
        hid[own_rows, cols] = (active * u).astype(BF)
        f1[:, cols] = u * sg * (1.0 + g * (1.0 - sg))
        f2[:, cols] = active
        return 0

    lax.fori_loop(0, FF // 256, forward, 0)
    gifts[2].start()
    ag_step(DOWN, 3)

    def rs(i, way, hop):
        sign = 1 - 2 * way
        lo, n = span_of(hop, way)
        rows = pl.ds(lo, n)
        src = s4.at[i, rows] if hop == 4 else sb.at[i, way, hop, rows]
        return pltpu.make_async_remote_copy(
            src_ref=src, dst_ref=sb.at[i, way, hop - 1, rows], send_sem=rs_s.at[i, way, hop - 1],
            recv_sem=rs_r.at[i, way, hop - 1], device_id={"dp": 2 * chip(sign) + c}, device_id_type=MESH)

    def term(i, k):
        left = yt if i == DOWN else xt
        right = (gcot, ucot, hid)[i]
        return nn(left[chip(k)], right[...])

    def rs_own(i, hop):
        if hop == 4:
            s4[i] = term(i, 4).astype(BF)
        elif hop == 0:
            tmp[0] = term(i, 0)
        else:
            tmp[0] = term(i, hop)
            tmp[1] = term(i, -hop)

    def rs_pass(i, hop):
        if hop == 4:
            rs(i, 0, 4).start()
            rs(i, 1, 4).start()
            return
        if hop == 0:
            for way in range(2):
                rs(i, way, 1).wait_recv()
            gr[i] = tmp[0] + sb[i, 0, 0].astype(F32) + sb[i, 1, 0].astype(F32)
            return
        for way in range(2):
            lo, n = span_of(hop + 1, way)
            rs(i, way, hop + 1).wait_recv()
            sb[i, way, hop, pl.ds(lo, n)] = (
                tmp[way, pl.ds(lo, n)] + sb[i, way, hop, pl.ds(lo, n)].astype(F32)).astype(BF)
            if n < SH:
                sb[i, way, hop, pl.ds(64 - lo, 64)] = tmp[way, pl.ds(64 - lo, 64)].astype(BF)
            rs(i, way, hop).start()

    def rs_step(i, hop):
        rs_own(i, hop)
        rs_pass(i, hop)

    gifts[1].wait_recv()
    gifts[2].wait_recv()
    rs_step(DOWN, 4)
    part(DOWN, yin, f3, (3,))

    def restack(first, second, dst, cols):
        for e in range(N):
            rows = slice(e * CAP, (e + 1) * CAP)
            dst[pl.ds(e * CH, CH), cols] = jnp.concatenate([first[rows], second[rows]], axis=0).astype(BF)

    def produce(k):
        left = hid[own_rows, :]
        restack(nt(left, w[DOWN, k]), nt(left, w[DOWN, k + 4]), xs, pl.ds(k * 256, 256))

    scatter_all(xs, gotx, rel_s.at[0], rel_r.at[0], "dp").wait_send()
    scatter_all(ys, goty, rel_s.at[1], rel_r.at[1], "dp").wait_send()
    rs_own(DOWN, 3)
    produce(1)
    ag_step(DOWN, 4)
    rs_pass(DOWN, 3)
    produce(2)
    shared(DOWN, 4).wait_recv()

    def backward(t, _):
        cols = pl.ds(pl.multiple_of(t * 256, 256), 256)
        hc = f3[:, cols] + chip_product(yin, DOWN, 4, cols)
        gcot[own_rows, cols] = (hc * f1[:, cols]).astype(BF)
        ucot[own_rows, cols] = (hc * f2[:, cols]).astype(BF)
        return 0

    lax.fori_loop(0, FF // 256, backward, 0)
    gifts[3].start()
    gifts[4].start()
    produce(3)
    produce(0)
    spread(xs, backo, bk_s.at[0], bk_r.at[0])
    gifts[0].wait_recv()
    gifts[3].wait_recv()
    rs_step(GATE, 4)
    gifts[4].wait_recv()
    rs_step(UP, 4)
    rs_step(DOWN, 2)

    def cotangent(k, _):
        lg, lu = gcot[own_rows, :], ucot[own_rows, :]
        parts = [nt(lg, w[GATE, k + 4 * h]) + nt(lu, w[UP, k + 4 * h]) for h in range(2)]
        restack(parts[0], parts[1], ys, pl.ds(pl.multiple_of(k * 256, 256), 256))
        return 0

    lax.fori_loop(0, HALF // 256, cotangent, 0)
    spread(ys, backd, bk_s.at[1], bk_r.at[1])

    stores = []

    def finish(i):
        rs_step(i, 0)
        cp = pltpu.make_async_copy(gr.at[i], (gg_hbm, gu_hbm, gd_hbm)[i].at[0], st.at[2 + i])
        cp.start()
        stores.append(cp)

    rs_step(GATE, 3)
    rs_step(UP, 3)
    rs_step(DOWN, 1)
    rs_step(GATE, 2)
    rs_step(UP, 2)
    finish(DOWN)

    def collect(i, src, dst):
        def body(t, _):
            cols = pl.ds(pl.multiple_of(t * 256, 256), 256)
            for h in range(2):
                at = pl.multiple_of(lax.rem(z + t + 4 * h, Z) * 256, 256)
                mo[i, :, pl.ds(at, 256)] = nn(sel[i, h], src[:, cols]).astype(BF)
            return 0
        lax.fori_loop(0, HALF // 256, body, 0)
        cp = pltpu.make_async_copy(mo.at[i], dst, st.at[i])
        cp.start()
        return cp

    scatter_all(xs, backo, bk_s.at[0], bk_r.at[0], "expert").wait_recv()
    stores.append(collect(0, backo, out_hbm))
    rs_step(GATE, 1)
    rs_step(UP, 1)
    finish(GATE)
    scatter_all(ys, backd, bk_s.at[1], bk_r.at[1], "expert").wait_recv()
    stores.append(collect(1, backd, dx_hbm))
    finish(UP)

    scatter_all(s2x, rcx, ex_s.at[0], ex_r.at[0], "expert").wait_send()
    scatter_all(s2y, rcy, ex_s.at[1], ex_r.at[1], "expert").wait_send()
    scatter_all(xs, backo, bk_s.at[0], bk_r.at[0], "expert").wait_send()
    scatter_all(ys, backd, bk_s.at[1], bk_r.at[1], "expert").wait_send()
    for g in gifts:
        g.wait_send()
    for i in range(3):
        for hop in range(5):
            shared(i, hop).wait_send()
        for way in range(2):
            for hop in range(1, 5):
                ag(i, way, hop).wait_send()
                rs(i, way, hop).wait_send()
    for cp in stores:
        cp.wait()


def hand_over(*refs):
    src, dst, held, sems = refs[:5], refs[5:10], refs[10:15], refs[15]
    reads = [pltpu.make_async_copy(src[i], held[i], sems.at[0, i]) for i in range(5)]
    writes = [pltpu.make_async_copy(held[i], dst[i], sems.at[1, i]) for i in range(5)]
    for cp in reads:
        cp.start()
    for i in range(5):
        reads[i].wait()
        writes[i].start()
    for cp in writes:
        cp.wait()


def local(attn_rows, out_grad, owner_rows, routes, gates, gate_weight, up_weight, down_weight):
    any_ = pl.BlockSpec(memory_space=pl.ANY)
    vm = pl.BlockSpec(memory_space=pltpu.VMEM)
    V, S = pltpu.VMEM, pltpu.SemaphoreType.DMA
    rows_t = V((STK, HALF), BF)
    scratch = [rows_t] * 12 + [
        V((3, Z, 2 * SH, FF), BF), V((STK, STK), BF), V((STK, STK), BF), V((3, STK, 2 * TOK), BF), V((2, 2, TOK, STK), BF),
        V((Z, SH, STK), BF), V((Z, SH, STK), BF), V((Z, SH, ROWS), BF), V((Z, SH, ROWS), BF),
        V((STK, FF), BF), V((STK, FF), BF), V((STK, FF), BF), V((ROWS, FF), F32), V((ROWS, FF), F32), V((ROWS, FF), F32),
        V((2, SH, FF), F32), V((3, SH, FF), BF), V((3, 2, 4, SH, FF), BF), V((2, TOK, D), BF), V((3, SH, FF), F32),
        S((7,)), S((2,)), S((2,)), S((2,)), S((2,)), S((2,)), S((2,)), S((3, 2, 4)), S((3, 2, 4)), S((3, 5)), S((3, 5)),
        S((5,)), S((5,)), S((3, 2, 4)), S((3, 2, 4)), S((5,)),
    ]
    grad = jax.ShapeDtypeStruct((1, SH, FF), F32)
    rows_o = jax.ShapeDtypeStruct((TOK, D), BF)
    results = pl.pallas_call(
        kernel,
        out_shape=(rows_o, rows_o, grad, grad, grad),
        in_specs=[any_, any_, pl.BlockSpec(memory_space=pltpu.SMEM), vm, vm, any_, any_, any_],
        out_specs=(any_,) * 5,
        scratch_shapes=scratch,
        compiler_params=pltpu.CompilerParams(collective_id=0, has_side_effects=True, vmem_limit_bytes=63 << 20),
        cost_estimate=pl.CostEstimate(flops=20_000_000_000, bytes_accessed=12_000_000, transcendentals=300_000),
    )(attn_rows, out_grad, owner_rows, routes.reshape(1, TOK), gates.reshape(1, TOK),
      gate_weight, up_weight, down_weight)
    return pl.pallas_call(
        hand_over,
        out_shape=(rows_o, rows_o, grad, grad, grad),
        in_specs=[any_] * 5,
        out_specs=(any_,) * 5,
        scratch_shapes=[V((TOK, D), BF), V((TOK, D), BF)] + [V((1, SH, FF), F32)] * 3 + [S((2, 5))],
    )(*results)


def solution(mesh):
    in_specs = (
        P(("dp", "expert"), None),
        P(("dp", "expert"), None),
        P("expert", None),
        P(("dp", "expert"), None),
        P(("dp", "expert")),
        P("expert", "dp", None),
        P("expert", "dp", None),
        P("expert", "dp", None),
    )
    out_specs = (
        P(("dp", "expert"), None),
        P(("dp", "expert"), None),
        P("expert", "dp", None),
        P("expert", "dp", None),
        P("expert", "dp", None),
    )
    return jax.shard_map(local, mesh=mesh, in_specs=in_specs, out_specs=out_specs, check_vma=False)
```

```python
import jax
import jax.numpy as jnp
from jax import lax
from jax.experimental import pallas as pl
from jax.experimental.pallas import tpu as pltpu
from jax.sharding import PartitionSpec as P

MESH = pl.DeviceIdType.MESH
BF = jnp.bfloat16
F32 = jnp.float32
N = 16
Z = 8
CAP = 24
CH = 2 * CAP
HALF = 1024
ROWS = N * CAP
STK = 2 * ROWS
TOK = 256
D = 2048
FF = 768
SH = 128
GATE, UP, DOWN = 0, 1, 2
PLANE = ((2, 2), (1, 3), (3, 1), (1, 1), (3, 3), (2, 1), (1, 2), (2, 3), (3, 2), (2, 0), (0, 2), (1, 0), (0, 1), (3, 0), (0, 3))


def nn(a, b):
    return jnp.dot(a, b, preferred_element_type=F32)


def nt(a, b):
    return lax.dot_general(a, b, (((1,), (1,)), ((), ())), preferred_element_type=F32)


def kernel(
    x_hbm, dy_hbm, lens_hbm, routes_hbm, gates_hbm, wg_hbm, wu_hbm, wd_hbm,
    out_hbm, dx_hbm, gg_hbm, gu_hbm, gd_hbm,
    lens, routes, gates, xin, yin, xs, ys, gotx, goty, s2x, s2y, rcx, rcy, backo, backd,
    w, perm, perm_g, a_t, sel,
    xt, yt, xt_s, yt_s, hid, gcot, ucot, f1, f2, f3, tmp, s4, sb, mo, gr,
    ld, rel_s, rel_r, ex_s, ex_r, bk_s, bk_r, ag_s, ag_r, sib_s, sib_r, act_s, act_r, rs_s, rs_r, st,
):
    dp = lax.axis_index("dp")
    ex = lax.axis_index("expert")
    z = dp // 2
    c = lax.rem(dp, 2)
    sibling = {"dp": dp + 1 - 2 * c}

    bar = pltpu.get_barrier_semaphore()

    def greet(i, _):
        pl.semaphore_signal(bar, 1, device_id={"dp": lax.rem(dp + i, N)}, device_id_type=MESH)
        pl.semaphore_signal(bar, 1, device_id={"expert": lax.rem(ex + i, N)}, device_id_type=MESH)
        return 0

    lax.fori_loop(1, N, greet, 0)

    loads = []
    for i, (src, dst) in enumerate(((x_hbm, xin), (dy_hbm, yin))):
        for h in range(2):
            loads.append(pltpu.make_async_copy(
                src.at[:, pl.ds(h * HALF, HALF)], dst.at[pl.ds(h * ROWS, ROWS)], ld.at[2 * i + h]))
    my_half = pl.ds(pl.multiple_of(c * SH, SH), SH)
    for i, src in enumerate((wg_hbm, wu_hbm, wd_hbm)):
        loads.append(pltpu.make_async_copy(src.at[0], w.at[i, 0, my_half], ld.at[4 + i]))
    for i, (src, dst) in enumerate(((lens_hbm, lens), (routes_hbm, routes), (gates_hbm, gates))):
        loads.append(pltpu.make_async_copy(src, dst, ld.at[7 + i]))
    for cp in loads[4:7] + loads[:4] + loads[7:]:
        cp.start()

    def permute(p_ref, src, dst):
        def body(t, _):
            cols = pl.ds(pl.multiple_of(t * 256, 256), 256)
            dst[:, cols] = nn(p_ref[...], src[:, cols]).astype(BF)
            return 0
        lax.fori_loop(0, HALF // 256, body, 0)

    def tile(i):
        return pl.ds(pl.multiple_of(i * CH, CH), CH)

    def scatter(src, dst, ssem, rsem, axis, me):
        def body(i, _):
            t = lax.rem(me + i, N)
            pltpu.make_async_remote_copy(
                src_ref=src.at[tile(t)], dst_ref=dst.at[tile(me)], send_sem=ssem, recv_sem=rsem,
                device_id={axis: t}, device_id_type=MESH).start()
            return 0
        lax.fori_loop(1, N, body, 0)
        dst[tile(me), :] = src[tile(me), :]

    def spread(src, dst, ssem, rsem):
        row, column = ex // 4, lax.rem(ex, 4)
        for a, b in PLANE:
            t = lax.rem(row + a, 4) * 4 + lax.rem(column + b, 4)
            pltpu.make_async_remote_copy(
                src_ref=src.at[tile(t)], dst_ref=dst.at[tile(ex)], send_sem=ssem, recv_sem=rsem,
                device_id={"expert": t}, device_id_type=MESH).start()
        dst[tile(ex), :] = src[tile(ex), :]

    def scatter_all(src, dst, ssem, rsem, axis):
        me = dp if axis == "dp" else ex
        span = pl.ds(0, (N - 1) * CH)
        return pltpu.make_async_remote_copy(
            src_ref=src.at[span], dst_ref=dst.at[span], send_sem=ssem, recv_sem=rsem,
            device_id={axis: lax.rem(me + 1, N)}, device_id_type=MESH)

    def span_of(hop, way):
        if hop < 4:
            return 0, SH
        return (0 if way == 0 else 64), 64

    def chip(k):
        return lax.rem(z + k + 2 * Z, Z)

    def ag(i, way, hop):
        sign = 1 - 2 * way
        lo, n = span_of(hop, way)
        rows = pl.ds(pl.multiple_of(c * SH + lo, 64), n)
        return pltpu.make_async_remote_copy(
            src_ref=w.at[i, (-sign * (hop - 1)) % Z, rows], dst_ref=w.at[i, (-sign * hop) % Z, rows],
            send_sem=ag_s.at[i, way, hop - 1], recv_sem=ag_r.at[i, way, hop - 1],
            device_id={"dp": 2 * chip(sign) + c}, device_id_type=MESH)

    def share(i, k, hop):
        block = w.at[i, k % Z, my_half]
        return pltpu.make_async_remote_copy(
            src_ref=block, dst_ref=block, send_sem=sib_s.at[i, hop], recv_sem=sib_r.at[i, hop],
            device_id=sibling, device_id_type=MESH)

    def shared(i, hop):
        block = w.at[i, hop, pl.ds(0, SH if hop in (0, 4) else 2 * SH)]
        return pltpu.make_async_remote_copy(
            src_ref=block, dst_ref=block, send_sem=sib_s.at[i, hop], recv_sem=sib_r.at[i, hop],
            device_id=sibling, device_id_type=MESH)

    def ag_step(i, hop):
        for way in range(2):
            ag(i, way, hop).wait_recv()
            if hop < 4:
                ag(i, way, hop + 1).start()
                share(i, (2 * way - 1) * hop, hop).start()
        if hop == 4:
            share(i, 4, 4).start()

    for i in range(3):
        loads[4 + i].wait()
    pl.semaphore_wait(bar, 2 * (N - 1))

    def ag_first(i):
        ag(i, 0, 1).start()
        ag(i, 1, 1).start()
        share(i, 0, 0).start()

    ag_first(GATE)
    ag_first(UP)
    loads[7].wait()
    def prefix(i, acc):
        return acc + jnp.where(i < dp, lens[0, i], 0)

    start = lax.fori_loop(0, N, prefix, jnp.int32(0))
    col = lax.broadcasted_iota(jnp.int32, (1, STK), 1)
    right_half = (col >= ROWS).astype(jnp.int32)
    r = col - ROWS * right_half
    dest = ((r + start) & (N - 1)) * CH + CAP * right_half + (r >> 4)
    row_iota = lax.broadcasted_iota(jnp.int32, (STK, STK), 0)
    perm[...] = jnp.where(row_iota == dest, 1.0, 0.0).astype(BF)

    loads[0].wait()
    loads[1].wait()
    permute(perm, xin, xs)
    scatter(xs, gotx, rel_s.at[0], rel_r.at[0], "dp", dp)
    loads[2].wait()
    loads[3].wait()
    permute(perm, yin, ys)
    scatter(ys, goty, rel_s.at[1], rel_r.at[1], "dp", dp)
    ag_first(DOWN)

    expert_iota = lax.broadcasted_iota(jnp.int32, (N, TOK), 0)
    loads[8].wait()
    loads[9].wait()
    route = routes[...]
    hot = expert_iota == route
    hot_f = jnp.where(hot, 1.0, 0.0)
    earlier = (lax.broadcasted_iota(jnp.int32, (TOK, TOK), 0) < lax.broadcasted_iota(jnp.int32, (TOK, TOK), 1))
    before = nn(hot_f.astype(BF), jnp.where(earlier, 1.0, 0.0).astype(BF))
    rank = jnp.sum(before * hot_f, axis=0, keepdims=True).astype(jnp.int32)
    slot = route * CH + rank
    pos = N * lax.broadcasted_iota(jnp.int32, (1, TOK), 1) + dp
    owner = jnp.zeros((1, TOK), jnp.int32)
    first = jnp.zeros((1, TOK), jnp.int32)
    end = jnp.int32(0)
    for b in range(N):
        end = end + lens[0, b]
        past = pos >= end
        owner = owner + jnp.where(past, 1, 0)
        first = jnp.where(past, end, first)
    got_row = owner * CH + ((pos - first) >> 4)
    gate_f = gates[...].astype(F32).reshape(1, TOK)
    tall = lax.broadcasted_iota(jnp.int32, (STK, TOK), 0)
    eye = jnp.where(
        lax.broadcasted_iota(jnp.int32, (TOK, TOK), 0) == lax.broadcasted_iota(jnp.int32, (TOK, TOK), 1), 1.0, 0.0
    ).astype(BF)
    for h in range(2):
        cols = pl.ds(h * TOK, TOK)
        hit = tall == slot + h * CAP
        plain = jnp.where(hit, 1.0, 0.0).astype(BF)
        gated = jnp.where(hit, gate_f, 0.0).astype(BF)
        a_t[0, :, cols] = plain
        a_t[1, :, cols] = gated
        a_t[2, :, cols] = jnp.where(tall == got_row + h * CAP, 1.0, 0.0).astype(BF)
        sel[0, h] = nt(eye, gated).astype(BF)
        sel[1, h] = nt(eye, plain).astype(BF)

    def build(t, _):
        rows = pl.ds(pl.multiple_of(t * 256, 256), 256)
        perm[rows, :] = nt(a_t[0, rows, :], a_t[2]).astype(BF)
        perm_g[rows, :] = nt(a_t[1, rows, :], a_t[2]).astype(BF)
        return 0

    lax.fori_loop(0, STK // 256, build, 0)

    def unstack(src, dst):
        def body(t, _):
            one = src[tile(2 * t), :].astype(F32)
            two = src[tile(2 * t + 1), :].astype(F32)
            at = pl.multiple_of(t * CH, CH)
            dst[pl.ds(at, CH), :] = jnp.concatenate([one[:CAP], two[:CAP]], axis=0).astype(BF)
            dst[pl.ds(at + ROWS, CH), :] = jnp.concatenate([one[CAP:], two[CAP:]], axis=0).astype(BF)
            return 0
        lax.fori_loop(0, N // 2, body, 0)

    own_rows = pl.ds(pl.multiple_of(c * ROWS, ROWS), ROWS)
    eye_s = eye[:SH, :SH]

    def turn(src, mine, theirs):
        def body(t, _):
            for par, dst in ((c, None), (1 - c, theirs)):
                d = 2 * t + par
                block = src[pl.ds(pl.multiple_of((d // Z) * ROWS, ROWS), ROWS),
                            pl.ds(pl.multiple_of(lax.rem(d, Z) * SH, SH), SH)]
                turned = nt(eye_s, block).astype(BF)
                if dst is None:
                    mine[t, :, own_rows] = turned
                else:
                    dst[t] = turned
            return 0
        lax.fori_loop(0, Z, body, 0)

    def give(i, src, dst):
        return pltpu.make_async_remote_copy(
            src_ref=src, dst_ref=dst, send_sem=act_s.at[i], recv_sem=act_r.at[i],
            device_id=sibling, device_id_type=MESH)

    gifts = (
        give(0, xt_s, xt.at[:, :, own_rows]),
        give(1, yt_s, yt.at[:, :, own_rows]),
        give(2, hid.at[own_rows], hid.at[own_rows]),
        give(3, gcot.at[own_rows], gcot.at[own_rows]),
        give(4, ucot.at[own_rows], ucot.at[own_rows]),
    )

    ag_step(GATE, 1)
    ag_step(UP, 1)
    scatter_all(xs, gotx, rel_s.at[0], rel_r.at[0], "dp").wait_recv()
    permute(perm, gotx, s2x)
    spread(s2x, rcx, ex_s.at[0], ex_r.at[0])
    scatter_all(ys, goty, rel_s.at[1], rel_r.at[1], "dp").wait_recv()
    permute(perm_g, goty, s2y)
    spread(s2y, rcy, ex_s.at[1], ex_r.at[1])
    ag_step(GATE, 2)
    scatter_all(s2x, rcx, ex_s.at[0], ex_r.at[0], "expert").wait_recv()
    unstack(rcx, xin)
    turn(xin, xt, xt_s)
    gifts[0].start()
    ag_step(UP, 2)
    ag_step(DOWN, 1)

    def chip_product(src, i, k, cols):
        o = chip(k)
        rows = src[pl.ds(pl.multiple_of((o // 4) * ROWS, ROWS), ROWS), pl.ds(pl.multiple_of(lax.rem(o, 4) * 256, 256), 256)]
        return nn(rows, w[i, k % Z, :, cols])

    def part(i, src, acc, hops):
        steps = []
        for hop in hops:
            shared(i, hop).wait_recv()
            steps += [hop] if hop in (0, 4) else [hop, -hop]
        for t in range(FF // 256):
            cols = pl.ds(t * 256, 256)
            total = chip_product(src, i, steps[0], cols)
            for k in steps[1:]:
                total = total + chip_product(src, i, k, cols)
            acc[:, cols] = total if 0 in hops else acc[:, cols] + total

    part(GATE, xin, f1, (0, 1))
    part(UP, xin, f2, (0, 1))
    ag_step(GATE, 3)
    part(GATE, xin, f1, (2,))
    part(UP, xin, f2, (2,))
    ag_step(UP, 3)
    scatter_all(s2y, rcy, ex_s.at[1], ex_r.at[1], "expert").wait_recv()
    unstack(rcy, yin)
    turn(yin, yt, yt_s)
    gifts[1].start()
    ag_step(DOWN, 2)
    part(GATE, xin, f1, (3,))
    part(UP, xin, f2, (3,))
    part(DOWN, yin, f3, (0, 1))
    ag_step(GATE, 4)
    ag_step(UP, 4)
    part(DOWN, yin, f3, (2,))
    shared(GATE, 4).wait_recv()
    shared(UP, 4).wait_recv()

    def forward(t, _):
        cols = pl.ds(pl.multiple_of(t * 256, 256), 256)
        g = f1[:, cols] + chip_product(xin, GATE, 4, cols)
        u = f2[:, cols] + chip_product(xin, UP, 4, cols)
        sg = jax.nn.sigmoid(g)
        active = g * sg
        hid[own_rows, cols] = (active * u).astype(BF)
        f1[:, cols] = u * sg * (1.0 + g * (1.0 - sg))
        f2[:, cols] = active
        return 0

    lax.fori_loop(0, FF // 256, forward, 0)
    gifts[2].start()
    ag_step(DOWN, 3)

    def rs(i, way, hop):
        sign = 1 - 2 * way
        lo, n = span_of(hop, way)
        rows = pl.ds(lo, n)
        src = s4.at[i, rows] if hop == 4 else sb.at[i, way, hop, rows]
        return pltpu.make_async_remote_copy(
            src_ref=src, dst_ref=sb.at[i, way, hop - 1, rows], send_sem=rs_s.at[i, way, hop - 1],
            recv_sem=rs_r.at[i, way, hop - 1], device_id={"dp": 2 * chip(sign) + c}, device_id_type=MESH)

    def term(i, k):
        left = yt if i == DOWN else xt
        right = (gcot, ucot, hid)[i]
        return nn(left[chip(k)], right[...])

    def rs_own(i, hop):
        if hop == 4:
            s4[i] = term(i, 4).astype(BF)
        elif hop == 0:
            tmp[0] = term(i, 0)
        else:
            tmp[0] = term(i, hop)
            tmp[1] = term(i, -hop)

    def rs_pass(i, hop):
        if hop == 4:
            rs(i, 0, 4).start()
            rs(i, 1, 4).start()
            return
        if hop == 0:
            for way in range(2):
                rs(i, way, 1).wait_recv()
            gr[i] = tmp[0] + sb[i, 0, 0].astype(F32) + sb[i, 1, 0].astype(F32)
            return
        for way in range(2):
            lo, n = span_of(hop + 1, way)
            rs(i, way, hop + 1).wait_recv()
            sb[i, way, hop, pl.ds(lo, n)] = (
                tmp[way, pl.ds(lo, n)] + sb[i, way, hop, pl.ds(lo, n)].astype(F32)).astype(BF)
            if n < SH:
                sb[i, way, hop, pl.ds(64 - lo, 64)] = tmp[way, pl.ds(64 - lo, 64)].astype(BF)
            rs(i, way, hop).start()

    def rs_step(i, hop):
        rs_own(i, hop)
        rs_pass(i, hop)

    gifts[1].wait_recv()
    gifts[2].wait_recv()
    rs_step(DOWN, 4)
    part(DOWN, yin, f3, (3,))

    def restack(first, second, dst, cols):
        for e in range(N):
            rows = slice(e * CAP, (e + 1) * CAP)
            dst[pl.ds(e * CH, CH), cols] = jnp.concatenate([first[rows], second[rows]], axis=0).astype(BF)

    def produce(k):
        left = hid[own_rows, :]
        restack(nt(left, w[DOWN, k]), nt(left, w[DOWN, k + 4]), xs, pl.ds(k * 256, 256))

    scatter_all(xs, gotx, rel_s.at[0], rel_r.at[0], "dp").wait_send()
    scatter_all(ys, goty, rel_s.at[1], rel_r.at[1], "dp").wait_send()
    rs_own(DOWN, 3)
    produce(1)
    ag_step(DOWN, 4)
    rs_pass(DOWN, 3)
    produce(2)
    shared(DOWN, 4).wait_recv()

    def backward(t, _):
        cols = pl.ds(pl.multiple_of(t * 256, 256), 256)
        hc = f3[:, cols] + chip_product(yin, DOWN, 4, cols)
        gcot[own_rows, cols] = (hc * f1[:, cols]).astype(BF)
        ucot[own_rows, cols] = (hc * f2[:, cols]).astype(BF)
        return 0

    lax.fori_loop(0, FF // 256, backward, 0)
    gifts[3].start()
    gifts[4].start()
    produce(3)
    produce(0)
    spread(xs, backo, bk_s.at[0], bk_r.at[0])
    gifts[0].wait_recv()
    gifts[3].wait_recv()
    rs_step(GATE, 4)
    gifts[4].wait_recv()
    rs_step(UP, 4)
    rs_step(DOWN, 2)

    def cotangent(k, _):
        lg, lu = gcot[own_rows, :], ucot[own_rows, :]
        parts = [nt(lg, w[GATE, k + 4 * h]) + nt(lu, w[UP, k + 4 * h]) for h in range(2)]
        restack(parts[0], parts[1], ys, pl.ds(pl.multiple_of(k * 256, 256), 256))
        return 0

    lax.fori_loop(0, HALF // 256, cotangent, 0)
    spread(ys, backd, bk_s.at[1], bk_r.at[1])

    stores = []

    def finish(i):
        rs_step(i, 0)
        cp = pltpu.make_async_copy(gr.at[i], (gg_hbm, gu_hbm, gd_hbm)[i].at[0], st.at[2 + i])
        cp.start()
        stores.append(cp)

    rs_step(GATE, 3)
    rs_step(UP, 3)
    rs_step(DOWN, 1)
    rs_step(GATE, 2)
    rs_step(UP, 2)
    finish(DOWN)

    def collect(i, src, dst):
        def body(t, _):
            cols = pl.ds(pl.multiple_of(t * 256, 256), 256)
            for h in range(2):
                at = pl.multiple_of(lax.rem(z + t + 4 * h, Z) * 256, 256)
                mo[i, :, pl.ds(at, 256)] = nn(sel[i, h], src[:, cols]).astype(BF)
            return 0
        lax.fori_loop(0, HALF // 256, body, 0)
        cp = pltpu.make_async_copy(mo.at[i], dst, st.at[i])
        cp.start()
        return cp

    scatter_all(xs, backo, bk_s.at[0], bk_r.at[0], "expert").wait_recv()
    stores.append(collect(0, backo, out_hbm))
    rs_step(GATE, 1)
    rs_step(UP, 1)
    finish(GATE)
    scatter_all(ys, backd, bk_s.at[1], bk_r.at[1], "expert").wait_recv()
    stores.append(collect(1, backd, dx_hbm))

    scatter_all(s2x, rcx, ex_s.at[0], ex_r.at[0], "expert").wait_send()
    scatter_all(s2y, rcy, ex_s.at[1], ex_r.at[1], "expert").wait_send()
    scatter_all(xs, backo, bk_s.at[0], bk_r.at[0], "expert").wait_send()
    scatter_all(ys, backd, bk_s.at[1], bk_r.at[1], "expert").wait_send()
    for g in gifts:
        g.wait_send()
    for i in range(3):
        for hop in range(5):
            shared(i, hop).wait_send()
        for way in range(2):
            for hop in range(1, 5):
                ag(i, way, hop).wait_send()
            for hop in range(2, 5):
                rs(i, way, hop).wait_send()
    finish(UP)
    for i in range(3):
        for way in range(2):
            rs(i, way, 1).wait_send()
    for cp in stores:
        cp.wait()


def hand_over(*refs):
    src, dst, held, sems = refs[:5], refs[5:10], refs[10:15], refs[15]
    pieces = [(i, pl.ds(r, 64)) for r in range(0, TOK, 64) for i in range(2)]
    pieces += [(i, pl.ds(0, 1)) for i in range(2, 5)]
    reads = [pltpu.make_async_copy(src[i].at[r], held[i].at[r], sems.at[0, n]) for n, (i, r) in enumerate(pieces)]
    writes = [pltpu.make_async_copy(held[i].at[r], dst[i].at[r], sems.at[1, n]) for n, (i, r) in enumerate(pieces)]
    for cp in reads:
        cp.start()
    for read, write in zip(reads, writes):
        read.wait()
        write.start()
    for cp in writes:
        cp.wait()


def local(attn_rows, out_grad, owner_rows, routes, gates, gate_weight, up_weight, down_weight):
    any_ = pl.BlockSpec(memory_space=pl.ANY)
    V, S = pltpu.VMEM, pltpu.SemaphoreType.DMA
    rows_t = V((STK, HALF), BF)
    scratch = [pltpu.SMEM((1, N), jnp.int32), V((1, TOK), jnp.int32), V((TOK,), BF)] + [rows_t] * 12 + [
        V((3, Z, 2 * SH, FF), BF), V((STK, STK), BF), V((STK, STK), BF), V((3, STK, 2 * TOK), BF), V((2, 2, TOK, STK), BF),
        V((Z, SH, STK), BF), V((Z, SH, STK), BF), V((Z, SH, ROWS), BF), V((Z, SH, ROWS), BF),
        V((STK, FF), BF), V((STK, FF), BF), V((STK, FF), BF), V((ROWS, FF), F32), V((ROWS, FF), F32), V((ROWS, FF), F32),
        V((2, SH, FF), F32), V((3, SH, FF), BF), V((3, 2, 4, SH, FF), BF), V((2, TOK, D), BF), V((3, SH, FF), F32),
        S((10,)), S((2,)), S((2,)), S((2,)), S((2,)), S((2,)), S((2,)), S((3, 2, 4)), S((3, 2, 4)), S((3, 5)), S((3, 5)),
        S((5,)), S((5,)), S((3, 2, 4)), S((3, 2, 4)), S((5,)),
    ]
    grad = jax.ShapeDtypeStruct((1, SH, FF), F32)
    rows_o = jax.ShapeDtypeStruct((TOK, D), BF)
    results = pl.pallas_call(
        kernel,
        out_shape=(rows_o, rows_o, grad, grad, grad),
        in_specs=[any_] * 8,
        out_specs=(any_,) * 5,
        scratch_shapes=scratch,
        compiler_params=pltpu.CompilerParams(collective_id=0, has_side_effects=True, vmem_limit_bytes=63 << 20),
        cost_estimate=pl.CostEstimate(flops=20_000_000_000, bytes_accessed=12_000_000, transcendentals=300_000),
    )(attn_rows, out_grad, owner_rows, routes.reshape(1, TOK), gates,
      gate_weight, up_weight, down_weight)
    return pl.pallas_call(
        hand_over,
        out_shape=(rows_o, rows_o, grad, grad, grad),
        in_specs=[any_] * 5,
        out_specs=(any_,) * 5,
        scratch_shapes=[V((TOK, D), BF), V((TOK, D), BF)] + [V((1, SH, FF), F32)] * 3 + [S((2, 11))],
    )(*results)


def solution(mesh):
    in_specs = (
        P(("dp", "expert"), None),
        P(("dp", "expert"), None),
        P("expert", None),
        P(("dp", "expert"), None),
        P(("dp", "expert")),
        P("expert", "dp", None),
        P("expert", "dp", None),
        P("expert", "dp", None),
    )
    out_specs = (
        P(("dp", "expert"), None),
        P(("dp", "expert"), None),
        P("expert", "dp", None),
        P("expert", "dp", None),
        P("expert", "dp", None),
    )
    return jax.shard_map(local, mesh=mesh, in_specs=in_specs, out_specs=out_specs, check_vma=False)
```

```python
import jax
import jax.numpy as jnp
from jax import lax
from jax.experimental import pallas as pl
from jax.experimental.pallas import tpu as pltpu
from jax.sharding import PartitionSpec as P

MESH = pl.DeviceIdType.MESH
BF = jnp.bfloat16
F32 = jnp.float32
N = 16
Z = 8
CAP = 24
CH = 2 * CAP
HALF = 1024
ROWS = N * CAP
STK = 2 * ROWS
TOK = 256
D = 2048
FF = 768
SH = 128
GATE, UP, DOWN = 0, 1, 2
PLANE = ((2, 2), (1, 3), (3, 1), (1, 1), (3, 3), (2, 1), (1, 2), (2, 3), (3, 2), (2, 0), (0, 2), (1, 0), (0, 1), (3, 0), (0, 3))


def nn(a, b):
    return jnp.dot(a, b, preferred_element_type=F32)


def nt(a, b):
    return lax.dot_general(a, b, (((1,), (1,)), ((), ())), preferred_element_type=F32)


def kernel(
    x_hbm, dy_hbm, lens_hbm, routes_hbm, gates_hbm, wg_hbm, wu_hbm, wd_hbm,
    out_hbm, dx_hbm, gg_hbm, gu_hbm, gd_hbm,
    lens, routes, gates, xin, yin, xs, ys, gotx, goty, s2x, s2y, rcx, rcy, backo, backd,
    w, perm, perm_g, a_t, sel,
    xt, yt, xt_s, yt_s, hid, gcot, ucot, f1, f2, f3, tmp, s4, sb, mo, gr,
    ld, rel_s, rel_r, ex_s, ex_r, bk_s, bk_r, ag_s, ag_r, sib_s, sib_r, act_s, act_r, rs_s, rs_r, st,
):
    dp = lax.axis_index("dp")
    ex = lax.axis_index("expert")
    z = dp // 2
    c = lax.rem(dp, 2)
    sibling = {"dp": dp + 1 - 2 * c}

    bar = pltpu.get_barrier_semaphore()

    def greet(i, _):
        pl.semaphore_signal(bar, 1, device_id={"dp": lax.rem(dp + i, N)}, device_id_type=MESH)
        pl.semaphore_signal(bar, 1, device_id={"expert": lax.rem(ex + i, N)}, device_id_type=MESH)
        return 0

    lax.fori_loop(1, N, greet, 0)

    loads = []
    for i, (src, dst) in enumerate(((x_hbm, xin), (dy_hbm, yin))):
        for h in range(2):
            loads.append(pltpu.make_async_copy(
                src.at[:, pl.ds(h * HALF, HALF)], dst.at[pl.ds(h * ROWS, ROWS)], ld.at[2 * i + h]))
    my_half = pl.ds(pl.multiple_of(c * SH, SH), SH)
    for i, src in enumerate((wg_hbm, wu_hbm, wd_hbm)):
        loads.append(pltpu.make_async_copy(src.at[0], w.at[i, 0, my_half], ld.at[4 + i]))
    for i, (src, dst) in enumerate(((lens_hbm, lens), (routes_hbm, routes), (gates_hbm, gates))):
        loads.append(pltpu.make_async_copy(src, dst, ld.at[7 + i]))
    for cp in loads[4:7] + loads[:4] + loads[7:]:
        cp.start()

    def permute(p_ref, src, dst):
        def body(t, _):
            cols = pl.ds(pl.multiple_of(t * 256, 256), 256)
            dst[:, cols] = nn(p_ref[...], src[:, cols]).astype(BF)
            return 0
        lax.fori_loop(0, HALF // 256, body, 0)

    def tile(i):
        return pl.ds(pl.multiple_of(i * CH, CH), CH)

    def scatter(src, dst, ssem, rsem, axis, me):
        def body(i, _):
            t = lax.rem(me + i, N)
            pltpu.make_async_remote_copy(
                src_ref=src.at[tile(t)], dst_ref=dst.at[tile(me)], send_sem=ssem, recv_sem=rsem,
                device_id={axis: t}, device_id_type=MESH).start()
            return 0
        lax.fori_loop(1, N, body, 0)
        dst[tile(me), :] = src[tile(me), :]

    def spread(src, dst, ssem, rsem):
        row, column = ex // 4, lax.rem(ex, 4)
        for a, b in PLANE:
            t = lax.rem(row + a, 4) * 4 + lax.rem(column + b, 4)
            pltpu.make_async_remote_copy(
                src_ref=src.at[tile(t)], dst_ref=dst.at[tile(ex)], send_sem=ssem, recv_sem=rsem,
                device_id={"expert": t}, device_id_type=MESH).start()
        dst[tile(ex), :] = src[tile(ex), :]

    def scatter_all(src, dst, ssem, rsem, axis):
        me = dp if axis == "dp" else ex
        span = pl.ds(0, (N - 1) * CH)
        return pltpu.make_async_remote_copy(
            src_ref=src.at[span], dst_ref=dst.at[span], send_sem=ssem, recv_sem=rsem,
            device_id={axis: lax.rem(me + 1, N)}, device_id_type=MESH)

    def span_of(hop, way):
        if hop < 4:
            return 0, SH
        return (0 if way == 0 else 64), 64

    def chip(k):
        return lax.rem(z + k + 2 * Z, Z)

    def ag(i, way, hop):
        sign = 1 - 2 * way
        lo, n = span_of(hop, way)
        rows = pl.ds(pl.multiple_of(c * SH + lo, 64), n)
        return pltpu.make_async_remote_copy(
            src_ref=w.at[i, (-sign * (hop - 1)) % Z, rows], dst_ref=w.at[i, (-sign * hop) % Z, rows],
            send_sem=ag_s.at[i, way, hop - 1], recv_sem=ag_r.at[i, way, hop - 1],
            device_id={"dp": 2 * chip(sign) + c}, device_id_type=MESH)

    def share(i, k, hop):
        block = w.at[i, k % Z, my_half]
        return pltpu.make_async_remote_copy(
            src_ref=block, dst_ref=block, send_sem=sib_s.at[i, hop], recv_sem=sib_r.at[i, hop],
            device_id=sibling, device_id_type=MESH)

    def shared(i, hop):
        block = w.at[i, hop, pl.ds(0, SH if hop in (0, 4) else 2 * SH)]
        return pltpu.make_async_remote_copy(
            src_ref=block, dst_ref=block, send_sem=sib_s.at[i, hop], recv_sem=sib_r.at[i, hop],
            device_id=sibling, device_id_type=MESH)

    def ag_step(i, hop):
        for way in range(2):
            ag(i, way, hop).wait_recv()
            if hop < 4:
                ag(i, way, hop + 1).start()
                share(i, (2 * way - 1) * hop, hop).start()
        if hop == 4:
            share(i, 4, 4).start()

    for i in range(3):
        loads[4 + i].wait()
    pl.semaphore_wait(bar, 2 * (N - 1))

    def ag_first(i):
        ag(i, 0, 1).start()
        ag(i, 1, 1).start()
        share(i, 0, 0).start()

    ag_first(GATE)
    ag_first(UP)
    loads[7].wait()
    def prefix(i, acc):
        return acc + jnp.where(i < dp, lens[0, i], 0)

    start = lax.fori_loop(0, N, prefix, jnp.int32(0))
    col = lax.broadcasted_iota(jnp.int32, (1, STK), 1)
    right_half = (col >= ROWS).astype(jnp.int32)
    r = col - ROWS * right_half
    dest = ((r + start) & (N - 1)) * CH + CAP * right_half + (r >> 4)
    row_iota = lax.broadcasted_iota(jnp.int32, (STK, STK), 0)
    perm[...] = jnp.where(row_iota == dest, 1.0, 0.0).astype(BF)

    loads[0].wait()
    loads[1].wait()
    permute(perm, xin, xs)
    scatter(xs, gotx, rel_s.at[0], rel_r.at[0], "dp", dp)
    loads[2].wait()
    loads[3].wait()
    permute(perm, yin, ys)
    scatter(ys, goty, rel_s.at[1], rel_r.at[1], "dp", dp)
    ag_first(DOWN)

    expert_iota = lax.broadcasted_iota(jnp.int32, (N, TOK), 0)
    loads[8].wait()
    loads[9].wait()
    route = routes[...]
    hot = expert_iota == route
    hot_f = jnp.where(hot, 1.0, 0.0)
    earlier = (lax.broadcasted_iota(jnp.int32, (TOK, TOK), 0) < lax.broadcasted_iota(jnp.int32, (TOK, TOK), 1))
    before = nn(hot_f.astype(BF), jnp.where(earlier, 1.0, 0.0).astype(BF))
    rank = jnp.sum(before * hot_f, axis=0, keepdims=True).astype(jnp.int32)
    slot = route * CH + rank
    pos = N * lax.broadcasted_iota(jnp.int32, (1, TOK), 1) + dp
    owner = jnp.zeros((1, TOK), jnp.int32)
    first = jnp.zeros((1, TOK), jnp.int32)
    end = jnp.int32(0)
    for b in range(N):
        end = end + lens[0, b]
        past = pos >= end
        owner = owner + jnp.where(past, 1, 0)
        first = jnp.where(past, end, first)
    got_row = owner * CH + ((pos - first) >> 4)
    gate_f = gates[...].astype(F32).reshape(1, TOK)
    tall = lax.broadcasted_iota(jnp.int32, (STK, TOK), 0)
    eye = jnp.where(
        lax.broadcasted_iota(jnp.int32, (TOK, TOK), 0) == lax.broadcasted_iota(jnp.int32, (TOK, TOK), 1), 1.0, 0.0
    ).astype(BF)
    for h in range(2):
        cols = pl.ds(h * TOK, TOK)
        hit = tall == slot + h * CAP
        plain = jnp.where(hit, 1.0, 0.0).astype(BF)
        gated = jnp.where(hit, gate_f, 0.0).astype(BF)
        a_t[0, :, cols] = plain
        a_t[1, :, cols] = gated
        a_t[2, :, cols] = jnp.where(tall == got_row + h * CAP, 1.0, 0.0).astype(BF)
        sel[0, h] = nt(eye, gated).astype(BF)
        sel[1, h] = nt(eye, plain).astype(BF)

    def build(t, _):
        rows = pl.ds(pl.multiple_of(t * 256, 256), 256)
        perm[rows, :] = nt(a_t[0, rows, :], a_t[2]).astype(BF)
        perm_g[rows, :] = nt(a_t[1, rows, :], a_t[2]).astype(BF)
        return 0

    lax.fori_loop(0, STK // 256, build, 0)

    def unstack(src, dst):
        def body(t, _):
            one = src[tile(2 * t), :].astype(F32)
            two = src[tile(2 * t + 1), :].astype(F32)
            at = pl.multiple_of(t * CH, CH)
            dst[pl.ds(at, CH), :] = jnp.concatenate([one[:CAP], two[:CAP]], axis=0).astype(BF)
            dst[pl.ds(at + ROWS, CH), :] = jnp.concatenate([one[CAP:], two[CAP:]], axis=0).astype(BF)
            return 0
        lax.fori_loop(0, N // 2, body, 0)

    own_rows = pl.ds(pl.multiple_of(c * ROWS, ROWS), ROWS)
    eye_s = eye[:SH, :SH]

    def turn(src, mine, theirs):
        def body(t, _):
            for par, dst in ((c, None), (1 - c, theirs)):
                d = 2 * t + par
                block = src[pl.ds(pl.multiple_of((d // Z) * ROWS, ROWS), ROWS),
                            pl.ds(pl.multiple_of(lax.rem(d, Z) * SH, SH), SH)]
                turned = nt(eye_s, block).astype(BF)
                if dst is None:
                    mine[t, :, own_rows] = turned
                else:
                    dst[t] = turned
            return 0
        lax.fori_loop(0, Z, body, 0)

    def give(i, src, dst):
        return pltpu.make_async_remote_copy(
            src_ref=src, dst_ref=dst, send_sem=act_s.at[i], recv_sem=act_r.at[i],
            device_id=sibling, device_id_type=MESH)

    gifts = (
        give(0, xt_s, xt.at[:, :, own_rows]),
        give(1, yt_s, yt.at[:, :, own_rows]),
        give(2, hid.at[own_rows], hid.at[own_rows]),
        give(3, gcot.at[own_rows], gcot.at[own_rows]),
        give(4, ucot.at[own_rows], ucot.at[own_rows]),
    )

    ag_step(GATE, 1)
    ag_step(UP, 1)
    scatter_all(xs, gotx, rel_s.at[0], rel_r.at[0], "dp").wait_recv()
    permute(perm, gotx, s2x)
    spread(s2x, rcx, ex_s.at[0], ex_r.at[0])
    scatter_all(ys, goty, rel_s.at[1], rel_r.at[1], "dp").wait_recv()
    permute(perm_g, goty, s2y)
    spread(s2y, rcy, ex_s.at[1], ex_r.at[1])
    ag_step(GATE, 2)
    scatter_all(s2x, rcx, ex_s.at[0], ex_r.at[0], "expert").wait_recv()
    unstack(rcx, xin)
    turn(xin, xt, xt_s)
    gifts[0].start()
    ag_step(UP, 2)
    ag_step(DOWN, 1)

    def chip_product(src, i, k, cols):
        o = chip(k)
        rows = src[pl.ds(pl.multiple_of((o // 4) * ROWS, ROWS), ROWS), pl.ds(pl.multiple_of(lax.rem(o, 4) * 256, 256), 256)]
        return nn(rows, w[i, k % Z, :, cols])

    def part(i, src, acc, hops):
        steps = []
        for hop in hops:
            shared(i, hop).wait_recv()
            steps += [hop] if hop in (0, 4) else [hop, -hop]
        for t in range(FF // 256):
            cols = pl.ds(t * 256, 256)
            total = chip_product(src, i, steps[0], cols)
            for k in steps[1:]:
                total = total + chip_product(src, i, k, cols)
            acc[:, cols] = total if 0 in hops else acc[:, cols] + total

    part(GATE, xin, f1, (0, 1))
    part(UP, xin, f2, (0, 1))
    ag_step(GATE, 3)
    part(GATE, xin, f1, (2,))
    part(UP, xin, f2, (2,))
    ag_step(UP, 3)
    scatter_all(s2y, rcy, ex_s.at[1], ex_r.at[1], "expert").wait_recv()
    unstack(rcy, yin)
    turn(yin, yt, yt_s)
    gifts[1].start()
    ag_step(DOWN, 2)
    part(GATE, xin, f1, (3,))
    part(UP, xin, f2, (3,))
    part(DOWN, yin, f3, (0, 1))
    ag_step(GATE, 4)
    ag_step(UP, 4)
    part(DOWN, yin, f3, (2,))
    shared(GATE, 4).wait_recv()
    shared(UP, 4).wait_recv()

    def forward(t, _):
        cols = pl.ds(t * 256, 256)
        g = f1[:, cols] + chip_product(xin, GATE, 4, cols)
        u = f2[:, cols] + chip_product(xin, UP, 4, cols)
        sg = jax.nn.sigmoid(g)
        active = g * sg
        hid[own_rows, cols] = (active * u).astype(BF)
        f1[:, cols] = u * sg * (1.0 + g * (1.0 - sg))
        f2[:, cols] = active
        give(2, hid.at[own_rows, cols], hid.at[own_rows, cols]).start()
        return 0

    for t in range(FF // 256):
        forward(t, 0)
    ag_step(DOWN, 3)

    def rs(i, way, hop):
        sign = 1 - 2 * way
        lo, n = span_of(hop, way)
        rows = pl.ds(lo, n)
        src = s4.at[i, rows] if hop == 4 else sb.at[i, way, hop, rows]
        return pltpu.make_async_remote_copy(
            src_ref=src, dst_ref=sb.at[i, way, hop - 1, rows], send_sem=rs_s.at[i, way, hop - 1],
            recv_sem=rs_r.at[i, way, hop - 1], device_id={"dp": 2 * chip(sign) + c}, device_id_type=MESH)

    def term(i, k):
        left = yt if i == DOWN else xt
        right = (gcot, ucot, hid)[i]
        return nn(left[chip(k)], right[...])

    def rs_own(i, hop):
        if hop == 4:
            s4[i] = term(i, 4).astype(BF)
        elif hop == 0:
            tmp[0] = term(i, 0)
        else:
            tmp[0] = term(i, hop)
            tmp[1] = term(i, -hop)

    def rs_pass(i, hop):
        if hop == 4:
            rs(i, 0, 4).start()
            rs(i, 1, 4).start()
            return
        if hop == 0:
            for way in range(2):
                rs(i, way, 1).wait_recv()
            gr[i] = tmp[0] + sb[i, 0, 0].astype(F32) + sb[i, 1, 0].astype(F32)
            return
        for way in range(2):
            lo, n = span_of(hop + 1, way)
            rs(i, way, hop + 1).wait_recv()
            sb[i, way, hop, pl.ds(lo, n)] = (
                tmp[way, pl.ds(lo, n)] + sb[i, way, hop, pl.ds(lo, n)].astype(F32)).astype(BF)
            if n < SH:
                sb[i, way, hop, pl.ds(64 - lo, 64)] = tmp[way, pl.ds(64 - lo, 64)].astype(BF)
            rs(i, way, hop).start()

    def rs_step(i, hop):
        rs_own(i, hop)
        rs_pass(i, hop)

    gifts[1].wait_recv()
    gifts[2].wait_recv()
    rs_step(DOWN, 4)
    part(DOWN, yin, f3, (3,))

    def restack(first, second, dst, cols):
        for e in range(N):
            rows = slice(e * CAP, (e + 1) * CAP)
            dst[pl.ds(e * CH, CH), cols] = jnp.concatenate([first[rows], second[rows]], axis=0).astype(BF)

    def produce(k):
        left = hid[own_rows, :]
        restack(nt(left, w[DOWN, k]), nt(left, w[DOWN, k + 4]), xs, pl.ds(k * 256, 256))

    scatter_all(xs, gotx, rel_s.at[0], rel_r.at[0], "dp").wait_send()
    scatter_all(ys, goty, rel_s.at[1], rel_r.at[1], "dp").wait_send()
    rs_own(DOWN, 3)
    produce(1)
    ag_step(DOWN, 4)
    rs_pass(DOWN, 3)
    produce(2)
    shared(DOWN, 4).wait_recv()

    def backward(t, _):
        cols = pl.ds(t * 256, 256)
        hc = f3[:, cols] + chip_product(yin, DOWN, 4, cols)
        gcot[own_rows, cols] = (hc * f1[:, cols]).astype(BF)
        ucot[own_rows, cols] = (hc * f2[:, cols]).astype(BF)
        give(3, gcot.at[own_rows, cols], gcot.at[own_rows, cols]).start()
        give(4, ucot.at[own_rows, cols], ucot.at[own_rows, cols]).start()
        return 0

    for t in range(FF // 256):
        backward(t, 0)
    produce(3)
    produce(0)
    spread(xs, backo, bk_s.at[0], bk_r.at[0])
    gifts[0].wait_recv()
    gifts[3].wait_recv()
    rs_step(GATE, 4)
    gifts[4].wait_recv()
    rs_step(UP, 4)
    rs_step(DOWN, 2)

    def cotangent(k, _):
        lg, lu = gcot[own_rows, :], ucot[own_rows, :]
        parts = [nt(lg, w[GATE, k + 4 * h]) + nt(lu, w[UP, k + 4 * h]) for h in range(2)]
        restack(parts[0], parts[1], ys, pl.ds(pl.multiple_of(k * 256, 256), 256))
        return 0

    lax.fori_loop(0, 2, cotangent, 0)
    rs_step(GATE, 3)
    lax.fori_loop(2, HALF // 256, cotangent, 0)
    spread(ys, backd, bk_s.at[1], bk_r.at[1])

    stores = []

    def finish(i):
        rs_step(i, 0)
        cp = pltpu.make_async_copy(gr.at[i], (gg_hbm, gu_hbm, gd_hbm)[i].at[0], st.at[2 + i])
        cp.start()
        stores.append(cp)

    rs_step(UP, 3)
    rs_step(DOWN, 1)
    rs_step(GATE, 2)
    rs_step(UP, 2)
    finish(DOWN)

    def collect(i, src, dst):
        def body(t, _):
            cols = pl.ds(pl.multiple_of(t * 256, 256), 256)
            for h in range(2):
                at = pl.multiple_of(lax.rem(z + t + 4 * h, Z) * 256, 256)
                mo[i, :, pl.ds(at, 256)] = nn(sel[i, h], src[:, cols]).astype(BF)
            return 0
        lax.fori_loop(0, HALF // 256, body, 0)
        cp = pltpu.make_async_copy(mo.at[i], dst, st.at[i])
        cp.start()
        return cp

    scatter_all(xs, backo, bk_s.at[0], bk_r.at[0], "expert").wait_recv()
    stores.append(collect(0, backo, out_hbm))
    rs_step(GATE, 1)
    rs_step(UP, 1)
    finish(GATE)
    scatter_all(ys, backd, bk_s.at[1], bk_r.at[1], "expert").wait_recv()
    stores.append(collect(1, backd, dx_hbm))

    scatter_all(s2x, rcx, ex_s.at[0], ex_r.at[0], "expert").wait_send()
    scatter_all(s2y, rcy, ex_s.at[1], ex_r.at[1], "expert").wait_send()
    scatter_all(xs, backo, bk_s.at[0], bk_r.at[0], "expert").wait_send()
    scatter_all(ys, backd, bk_s.at[1], bk_r.at[1], "expert").wait_send()
    for g in gifts:
        g.wait_send()
    for i in range(3):
        for hop in range(5):
            shared(i, hop).wait_send()
        for way in range(2):
            for hop in range(1, 5):
                ag(i, way, hop).wait_send()
            for hop in range(2, 5):
                rs(i, way, hop).wait_send()
    finish(UP)
    for i in range(3):
        for way in range(2):
            rs(i, way, 1).wait_send()
    for cp in stores:
        cp.wait()


def hand_over(*refs):
    src, dst, held, sems = refs[:5], refs[5:10], refs[10:15], refs[15]
    pieces = [(i, pl.ds(r, 64)) for r in range(0, TOK, 64) for i in range(2)]
    pieces += [(i, pl.ds(0, 1)) for i in range(2, 5)]
    reads = [pltpu.make_async_copy(src[i].at[r], held[i].at[r], sems.at[0, n]) for n, (i, r) in enumerate(pieces)]
    writes = [pltpu.make_async_copy(held[i].at[r], dst[i].at[r], sems.at[1, n]) for n, (i, r) in enumerate(pieces)]
    for cp in reads:
        cp.start()
    for read, write in zip(reads, writes):
        read.wait()
        write.start()
    for cp in writes:
        cp.wait()


def local(attn_rows, out_grad, owner_rows, routes, gates, gate_weight, up_weight, down_weight):
    any_ = pl.BlockSpec(memory_space=pl.ANY)
    V, S = pltpu.VMEM, pltpu.SemaphoreType.DMA
    rows_t = V((STK, HALF), BF)
    scratch = [pltpu.SMEM((1, N), jnp.int32), V((1, TOK), jnp.int32), V((TOK,), BF)] + [rows_t] * 12 + [
        V((3, Z, 2 * SH, FF), BF), V((STK, STK), BF), V((STK, STK), BF), V((3, STK, 2 * TOK), BF), V((2, 2, TOK, STK), BF),
        V((Z, SH, STK), BF), V((Z, SH, STK), BF), V((Z, SH, ROWS), BF), V((Z, SH, ROWS), BF),
        V((STK, FF), BF), V((STK, FF), BF), V((STK, FF), BF), V((ROWS, FF), F32), V((ROWS, FF), F32), V((ROWS, FF), F32),
        V((2, SH, FF), F32), V((3, SH, FF), BF), V((3, 2, 4, SH, FF), BF), V((2, TOK, D), BF), V((3, SH, FF), F32),
        S((10,)), S((2,)), S((2,)), S((2,)), S((2,)), S((2,)), S((2,)), S((3, 2, 4)), S((3, 2, 4)), S((3, 5)), S((3, 5)),
        S((5,)), S((5,)), S((3, 2, 4)), S((3, 2, 4)), S((5,)),
    ]
    grad = jax.ShapeDtypeStruct((1, SH, FF), F32)
    rows_o = jax.ShapeDtypeStruct((TOK, D), BF)
    results = pl.pallas_call(
        kernel,
        out_shape=(rows_o, rows_o, grad, grad, grad),
        in_specs=[any_] * 8,
        out_specs=(any_,) * 5,
        scratch_shapes=scratch,
        compiler_params=pltpu.CompilerParams(collective_id=0, has_side_effects=True, vmem_limit_bytes=63 << 20),
        cost_estimate=pl.CostEstimate(flops=20_000_000_000, bytes_accessed=12_000_000, transcendentals=300_000),
    )(attn_rows, out_grad, owner_rows, routes.reshape(1, TOK), gates,
      gate_weight, up_weight, down_weight)
    return pl.pallas_call(
        hand_over,
        out_shape=(rows_o, rows_o, grad, grad, grad),
        in_specs=[any_] * 5,
        out_specs=(any_,) * 5,
        scratch_shapes=[V((TOK, D), BF), V((TOK, D), BF)] + [V((1, SH, FF), F32)] * 3 + [S((2, 11))],
    )(*results)


def solution(mesh):
    in_specs = (
        P(("dp", "expert"), None),
        P(("dp", "expert"), None),
        P("expert", None),
        P(("dp", "expert"), None),
        P(("dp", "expert")),
        P("expert", "dp", None),
        P("expert", "dp", None),
        P("expert", "dp", None),
    )
    out_specs = (
        P(("dp", "expert"), None),
        P(("dp", "expert"), None),
        P("expert", "dp", None),
        P("expert", "dp", None),
        P("expert", "dp", None),
    )
    return jax.shard_map(local, mesh=mesh, in_specs=in_specs, out_specs=out_specs, check_vma=False)
```
